32 devices in a mesh: groups: 2 (over y), seq: 16 (over z, x, core).
Axes of the slice: x: 2, y: 2, z: 4, core: 2. Of those that a mesh axis runs over, the one named last changes fastest.
Arguments:
- projected: bfloat16 [4096, 6144], P(('groups', 'seq')), parts along dimension 0, may hold values from -6 to 6
- filters: float32 [3, 7, 2048], replicated, may hold values from -3 to 3
- upstream: bfloat16 [4096, 2048], P(('groups', 'seq')), parts along dimension 0, may hold values from -20 to 20
Outputs:
- gated: bfloat16 [4096, 2048], P(('groups', 'seq')), parts along dimension 0
- grad_projected: bfloat16 [4096, 6144], P(('groups', 'seq')), parts along dimension 0
- grad_filters: float32 [6, 7, 2048], P('groups'), parts along dimension 0
The draws below stay inside these ranges and needn't reach their ends.
There are 2 independent parts, one for each index of `groups`. The reference program is written for one: setup_inputs(seed, part) draws one part's arguments, and reference() takes and returns one part's arrays. A program takes and returns all parts, laid end to end along the dimension named above; an argument that names none is the same for every part. Nothing has to cross between parts.
All inputs are finite; a program needn't handle non-finite values.
Results may differ from the reference program's by a relative error of at most 0.005.
Values may be sent and summed in bfloat16 or wider, within the bound.
No kernel may reach another device: no remote copies, remote signals or barrier semaphores. Data moves between devices by JAX's collectives and lax.ppermute only.
A program may use at most 64 MiB of HBM per device.

```python
import jax
import jax.numpy as jnp

CH = 2048
TAPS = 7
TOKENS = 2048


def draw_upstream(key, part):
    key = jax.random.fold_in(key, 11)
    position = jnp.arange(TOKENS, dtype=jnp.float32)[:, None] / float(TOKENS - 1)
    base = jnp.clip(jax.random.normal(key, (TOKENS, CH), jnp.float32), -4.0, 4.0)
    return (base * (1.0 + 2.0 * position)).astype(jnp.bfloat16)


def block_scale(stream_key, extent, cuts, least, high):
    loudness = 1.0
    for dim, shards_of in cuts:
        draws = jax.random.uniform(jax.random.fold_in(jax.random.fold_in(stream_key, 6), dim), (shards_of,), jnp.float32, least / len(cuts), high / len(cuts))
        loudness = loudness * jnp.repeat(jnp.exp(draws), extent[dim] // shards_of).reshape((-1,) + (1,) * (len(extent) - 1 - dim))
    return loudness


def scatter_about(key, extent, scale, reach, cuts=(), kind=jnp.bfloat16):
    array = jax.random.normal(key, extent, jnp.float32) * scale
    if len(cuts) > 0:
        array = block_scale(key, extent, cuts, -0.22, 0.18) * array
    return jnp.clip(array, min=-reach, max=reach).astype(kind)


def setup_inputs(seed: int = 0, part: int = 0) -> dict:
    splits = jax.random.split(jax.random.key(seed), 4)
    part_keys = jax.random.split(jax.random.fold_in(splits[3], part), 4)
    return {
        "projected": scatter_about(part_keys[0], (TOKENS, 3 * CH), 1.0, 6.0, ((0, 16),)),
        "filters": scatter_about(splits[1], (3, TAPS, CH), 0.5, 3.0, (), jnp.float32),
        "upstream": draw_upstream(jax.random.fold_in(jax.random.fold_in(splits[3], part), 71), part),
    }


def causal_filter(values, tap_table):
    length = values.shape[0]
    rim_rows = TAPS - 1
    padded = jnp.concatenate([jnp.zeros((rim_rows, values.shape[1]), jnp.float32), values], 0)
    result = jnp.zeros(values.shape, jnp.float32)
    for tap_index in range(TAPS):
        result = result + tap_table[tap_index] * padded[rim_rows - tap_index:rim_rows - tap_index + length]
    return result, padded


def reference(projected, filters, upstream):
    rim_rows = TAPS - 1
    scale = float(TOKENS) ** -0.5
    tap_table = jnp.transpose(filters, (1, 0, 2)).reshape(TAPS, 3 * CH)
    convolved, padded = causal_filter(projected.astype(jnp.float32), tap_table)
    query = convolved[:, :CH]
    keys = convolved[:, CH:2 * CH]
    values = convolved[:, 2 * CH:]
    gated = (query * keys * values).astype(jnp.bfloat16)
    cotangent = upstream.astype(jnp.float32)
    grad_conv = jnp.concatenate([cotangent * keys * values, cotangent * query * values, cotangent * query * keys], 1).astype(jnp.bfloat16)
    grad_float = grad_conv.astype(jnp.float32)
    length = grad_float.shape[0]
    grad_padded = jnp.concatenate([grad_float, jnp.zeros((rim_rows, 3 * CH), jnp.float32)], 0)
    grad_proj = jnp.zeros(grad_float.shape, jnp.float32)
    tap_grads = []
    for tap_index in range(TAPS):
        grad_proj = grad_proj + tap_table[tap_index] * grad_padded[tap_index:tap_index + length]
        tap_grads.append(jnp.sum(grad_float * padded[rim_rows - tap_index:rim_rows - tap_index + length], 0))
    grad_projected = grad_proj.astype(jnp.bfloat16)
    grad_taps = jnp.stack(tap_grads, 0) * scale
    grad_filters = jnp.transpose(grad_taps.reshape(TAPS, 3, CH), (1, 0, 2))
    return gated, grad_projected, grad_filters
```

```python
import jax, jax.numpy as jnp
from jax import lax
from jax.experimental import pallas as pl
from jax.experimental.pallas import tpu as pltpu
from jax.sharding import PartitionSpec as P

F32 = jnp.float32
BF = jnp.bfloat16
L = 128
SUB = 8
RIM = 8
def filter_kernel(p_ref, u_ref, f_ref, prior_ref, next_ref, gated_ref, g_ref, taps_ref, p_slab, u_slab, o_slab):
    rows, columns = p_ref.shape
    chans = columns // 3
    taps = f_ref.shape[1]
    pitch = rows // SUB
    half = chans // 2
    def group(n, carry):
        col = pl.multiple_of(n * L, L)
        for s in range(3):
            c = pl.multiple_of(s * chans + n * L, L)
            p_slab[s, 0:8, :] = prior_ref[:, pl.ds(c, L)].astype(F32)
            p_slab[s, 8:8 + rows, :] = p_ref[:, pl.ds(c, L)].astype(F32)
            p_slab[s, 8 + rows:16 + rows, :] = next_ref[:, pl.ds(c, L)].astype(F32)
        u_slab[...] = u_ref[:, pl.ds(col, L)].astype(F32)
        tap = [[jnp.broadcast_to(f_ref[s, j:j + 1, pl.ds(col, L)], (SUB, L)) for j in range(taps)] for s in range(3)]
        window = [[p_slab[s, pl.ds(8 + r, SUB, stride=pitch), :] for r in range(1 - taps, 0)] for s in range(3)]
        for r in range(pitch):
            conv = []
            for s in range(3):
                window[s].append(p_slab[s, pl.ds(8 + r, SUB, stride=pitch), :])
                w = window[s]
                conv.append(sum(tap[s][j] * w[-1 - j] for j in range(taps)))
                window[s] = w[1:]
            u = u_slab[pl.ds(r, SUB, stride=pitch), :]
            q, k, v = conv
            kv = k * v
            uq = u * q
            o_slab[pl.ds(r, SUB, stride=pitch), :] = q * kv
            for s, g in enumerate((u * kv, uq * v, uq * k)):
                g_ref[s, n, pl.ds(r, SUB, stride=pitch), :] = g.astype(BF).astype(F32)
        gated_ref[:, pl.ds(col, L)] = o_slab[...].astype(BF)
        un = next_ref[:, pl.ds(pl.multiple_of(columns + n * L, L), L)].astype(F32)
        conv = [sum(tap[s][j] * p_slab[s, 8 + rows - j:16 + rows - j, :] for j in range(taps)) for s in range(3)]
        q, k, v = conv
        for s, g in enumerate((un * (k * v), un * q * v, un * q * k)):
            g_ref[s, n, rows:rows + 8, :] = g.astype(BF).astype(F32)
        h = n // (half // L)
        hcol = pl.multiple_of((n % (half // L)) * L, L)
        for s in range(3):
            w = [p_slab[s, pl.ds(8 + r, SUB, stride=pitch), :] for r in range(1 - taps, 0)]
            acc = [jnp.zeros((SUB, L), F32)] * taps
            for r in range(pitch):
                w.append(p_slab[s, pl.ds(8 + r, SUB, stride=pitch), :])
                g = g_ref[s, n, pl.ds(r, SUB, stride=pitch), :]
                acc = [acc[j] + g * w[-1 - j] for j in range(taps)]
                w = w[1:]
            for j in range(taps):
                taps_ref[h, 8 * s + j:8 * s + j + 1, pl.ds(hcol, L)] = jnp.sum(acc[j], 0, keepdims=True)
            taps_ref[h, 8 * s + taps:8 * s + 8, pl.ds(hcol, L)] = jnp.zeros((8 - taps, L), F32)
        return carry
    lax.fori_loop(0, chans // L, group, 0)

def back_kernel(f_ref, g_ref, out_ref, o_slab):
    rows, columns = out_ref.shape
    chans = columns // 3
    taps = f_ref.shape[1]
    pitch = rows // SUB
    def group(n, carry):
        col = pl.multiple_of(n * L, L)
        for s in range(3):
            tap = [jnp.broadcast_to(f_ref[s, j:j + 1, pl.ds(col, L)], (SUB, L)) for j in range(taps)]
            w = [g_ref[s, n, pl.ds(r, SUB, stride=pitch), :] for r in range(taps - 1)]
            for r in range(pitch):
                w.append(g_ref[s, n, pl.ds(r + taps - 1, SUB, stride=pitch), :])
                o_slab[s, pl.ds(r, SUB, stride=pitch), :] = sum(tap[j] * w[j] for j in range(taps))
                w = w[1:]
            out_ref[:, pl.ds(pl.multiple_of(s * chans + n * L, L), L)] = o_slab[s].astype(BF)
        return carry
    lax.fori_loop(0, chans // L, group, 0)

V = pl.BlockSpec(memory_space=pltpu.VMEM)
def call_filter(p, u, f, prior, nxt):
    rows, columns = p.shape; chans = columns // 3
    return pl.pallas_call(filter_kernel,
        out_shape=(jax.ShapeDtypeStruct((rows, chans), BF), jax.ShapeDtypeStruct((3, chans // L, rows + 8, L), F32), jax.ShapeDtypeStruct((2, 24, chans // 2), F32)),
        in_specs=[V]*5, out_specs=(V, V, V),
        scratch_shapes=[pltpu.VMEM((3, rows + 16, L), F32), pltpu.VMEM((rows, L), F32), pltpu.VMEM((rows, L), F32)],
        cost_estimate=pl.CostEstimate(flops=2*2*7*rows*columns, bytes_accessed=2*rows*(columns+chans), transcendentals=0),
        compiler_params=pltpu.CompilerParams(vmem_limit_bytes=24*2**20), name="filter")(p, u, f, prior, nxt)
def call_back(f, g, rows, columns):
    return pl.pallas_call(back_kernel, out_shape=jax.ShapeDtypeStruct((rows, columns), BF),
        in_specs=[V]*2, out_specs=V, scratch_shapes=[pltpu.VMEM((3, rows, L), F32)],
        cost_estimate=pl.CostEstimate(flops=2*7*rows*columns, bytes_accessed=2*rows*columns, transcendentals=0),
        compiler_params=pltpu.CompilerParams(vmem_limit_bytes=24*2**20), name="back")(f, g)


def swap(array, partner):
    ways = lax.axis_size("seq")
    return lax.ppermute(array, "seq", [(i, partner(i)) for i in range(ways)])


def rims(projected, upstream):
    rows, columns = projected.shape
    chans = upstream.shape[1]
    ways = lax.axis_size("seq")
    me = lax.axis_index("seq")
    even = me % 2 == 0
    first = jnp.concatenate([projected[:RIM], upstream[:RIM]], 1)
    last = jnp.concatenate([projected[rows - RIM :], jnp.zeros((RIM, chans), BF)], 1)
    far = swap(jnp.where(even, first, last), lambda i: (((i + 1) % ways) ^ 1) - 1 if 0 < i < ways - 1 else ways - 1 - i)
    near = swap(jnp.where(even, last, first), lambda i: i ^ 1)
    before = jnp.where(even, far, near)[:, :columns]
    after = jnp.where(even, near, far)
    before = jnp.where(me == 0, jnp.zeros_like(before), before)
    after = jnp.where(me == ways - 1, jnp.zeros_like(after), after)
    return before, after


def total_over_seq(halves):
    ways = lax.axis_size("seq")
    me = lax.axis_index("seq")
    bits = ways.bit_length() - 1
    odd = sum((me >> b) & 1 for b in range(bits)) % 2 == 1
    mine = jnp.where(odd, halves[1], halves[0])
    other = jnp.where(odd, halves[0], halves[1])
    mine = mine + swap(other, lambda i: i ^ 1)
    for b in range(1, bits):
        sent = mine.astype(BF)
        mine = sent.astype(F32) + swap(sent, lambda i: i ^ (1 << b) ^ 1).astype(F32)
    other = swap(mine, lambda i: i ^ 1)
    return jnp.where(odd, other, mine), jnp.where(odd, mine, other)


def shards(projected, filters, upstream):
    rows, columns = projected.shape
    ways = lax.axis_size("seq")
    taps = filters.shape[1]
    chans = columns // 3
    before, after = rims(projected, upstream)
    gated, grad_conv, tap_grads = call_filter(projected, upstream, filters, before, after)
    low, high = total_over_seq(tap_grads)
    grad_projected = call_back(filters, grad_conv, rows, columns)
    total = jnp.concatenate([low, high], 1).reshape(3, 8, chans)[:, :taps]
    return gated, grad_projected, total * float(rows * ways) ** -0.5


def solution(mesh):
    placed = (P(("groups", "seq"), None), P(), P(("groups", "seq"), None))
    return jax.shard_map(
        shards,
        mesh=mesh,
        in_specs=placed,
        out_specs=(P(("groups", "seq"), None), P(("groups", "seq"), None), P("groups", None, None)),
        check_vma=False,
    )
```

```python
import jax
import jax.numpy as jnp
from jax import lax
from jax.experimental import pallas as pl
from jax.experimental.pallas import tpu as pltpu
from jax.sharding import PartitionSpec as P

F32 = jnp.float32
BF = jnp.bfloat16
LANES = 128
SUB = 8
RIM = 8
VMEM = pl.BlockSpec(memory_space=pltpu.VMEM)
UNROLL = 4


def lanes_at(start):
    return pl.ds(pl.multiple_of(start, LANES), LANES)


def tap_rows(filters, s, n):
    return [
        jnp.broadcast_to(filters[s, j : j + 1, lanes_at(n * LANES)], (SUB, LANES))
        for j in range(filters.shape[1])
    ]


def convolve(tap, slab, s, start):
    return sum(tap[s][j] * slab[s, start - j : start - j + SUB, :] for j in range(len(tap[s])))


def gates(query, key, value, cotangent):
    product = key * value
    scaled = cotangent * query
    grads = (cotangent * product, scaled * value, scaled * key)
    return query * product, [g.astype(BF).astype(F32) for g in grads]


def inner_kernel(p_ref, u_ref, filters, gated, grads, sums, p_slab, u_slab):
    rows, columns = p_ref.shape
    chans = columns // 3
    taps = filters.shape[1]

    def group(n, carry):
        for s in range(3):
            p_slab[s] = p_ref[:, lanes_at(s * chans + n * LANES)].astype(F32)
        u_slab[...] = u_ref[:, lanes_at(n * LANES)].astype(F32)
        tap = [tap_rows(filters, s, n) for s in range(3)]
        for r in range(RIM, rows, SUB):
            conv = [convolve(tap, p_slab, s, r) for s in range(3)]
            product, grad = gates(*conv, u_slab[r : r + SUB, :])
            gated[n, r : r + SUB, :] = product
            for s in range(3):
                grads[s, n, r : r + SUB, :] = grad[s]
        for s in range(3):
            acc = [None] * taps
            for r in range(RIM, rows, SUB):
                grad = grads[s, n, r : r + SUB, :]
                for j in range(taps):
                    term = grad * p_slab[s, r - j : r - j + SUB, :]
                    acc[j] = term if r == RIM else acc[j] + term
            for j in range(taps):
                sums[n, s, j] = acc[j]
        return carry

    lax.fori_loop(0, chans // LANES, group, 0, unroll=UNROLL)


def fold(arrays):
    sub = lax.broadcasted_iota(jnp.int32, (SUB, LANES), 0)
    arrays = arrays + [jnp.zeros((SUB, LANES), F32)] * (SUB - len(arrays))
    step = 1
    while step < SUB:
        low = (sub & step) == 0
        arrays = [
            jnp.where(low, a, b) + pltpu.roll(jnp.where(low, b, a), SUB - step, 0)
            for a, b in zip(arrays[::2], arrays[1::2])
        ]
        step *= 2
    return arrays[0]


def rim_kernel(p_ref, u_ref, filters, before, after, sums, gated, head, following, totals, slab):
    rows, columns = p_ref.shape
    chans = columns // 3
    taps = filters.shape[1]
    half = chans // 2 // LANES

    def group(n, carry):
        for s in range(3):
            c = lanes_at(s * chans + n * LANES)
            slab[s, 0:RIM, :] = before[:, c].astype(F32)
            slab[s, RIM : RIM + 16, :] = p_ref[0:16, c].astype(F32)
            slab[s, RIM + 16 : RIM + 32, :] = p_ref[rows - 16 : rows, c].astype(F32)
            slab[s, RIM + 32 : RIM + 40, :] = after[:, c].astype(F32)
        tap = [tap_rows(filters, s, n) for s in range(3)]
        conv = [convolve(tap, slab, s, RIM + 32) for s in range(3)]
        _, grad = gates(*conv, after[:, lanes_at(columns + n * LANES)].astype(F32))
        for s in range(3):
            following[s, n] = grad[s]
        conv = [convolve(tap, slab, s, RIM) for s in range(3)]
        product, grad = gates(*conv, u_ref[0:16, lanes_at(n * LANES)].astype(F32)[0:RIM])
        gated[n] = product
        c = lanes_at(lax.rem(n, half) * LANES)
        for s in range(3):
            head[s, n] = grad[s]
            acc = [sums[n, s, j] + grad[s] * slab[s, RIM - j : RIM - j + SUB, :] for j in range(taps)]
            totals[n // half, s * SUB : s * SUB + SUB, c] = fold(acc)
        return carry

    lax.fori_loop(0, chans // LANES, group, 0, unroll=UNROLL)


def back_kernel(filters, gated_in, grads, gated_head, head, following, gated, out, slab):
    rows, columns = out.shape
    chans = columns // 3
    taps = filters.shape[1]

    def group(n, carry):
        c = lanes_at(n * LANES)
        gated[0:16, c] = jnp.concatenate([gated_head[n], gated_in[n, RIM:16, :]], 0).astype(BF)
        gated[16:rows, c] = gated_in[n, 16:rows, :].astype(BF)
        for s in range(3):
            tap = tap_rows(filters, s, n)
            slab[s, 0:RIM, :] = head[s, n]
            slab[s, RIM : 2 * RIM, :] = grads[s, n, RIM : 2 * RIM, :]
            slab[s, 2 * RIM : 3 * RIM, :] = grads[s, n, rows - RIM : rows, :]
            slab[s, 3 * RIM : 4 * RIM, :] = following[s, n]
            result = []
            for r in range(0, rows, SUB):
                if r == 0:
                    terms = [tap[j] * slab[s, j : j + SUB, :] for j in range(taps)]
                elif r == rows - SUB:
                    terms = [tap[j] * slab[s, 2 * RIM + j : 2 * RIM + j + SUB, :] for j in range(taps)]
                else:
                    terms = [tap[j] * grads[s, n, r + j : r + j + SUB, :] for j in range(taps)]
                result.append(sum(terms))
                if r % 16 == SUB:
                    out[r - SUB : r + SUB, lanes_at(s * chans + n * LANES)] = jnp.concatenate(result, 0).astype(BF)
                    result = []
        return carry

    lax.fori_loop(0, chans // LANES, group, 0, unroll=UNROLL)


def params(**kw):
    return pltpu.CompilerParams(vmem_limit_bytes=28 * 2**20, **kw)


def call_inner(projected, upstream, filters):
    rows, columns = projected.shape
    chans = columns // 3
    groups = chans // LANES
    taps = filters.shape[1]
    return pl.pallas_call(
        inner_kernel,
        out_shape=(
            jax.ShapeDtypeStruct((groups, rows, LANES), F32),
            jax.ShapeDtypeStruct((3, groups, rows, LANES), F32),
            jax.ShapeDtypeStruct((groups, 3, taps, SUB, LANES), F32),
        ),
        in_specs=[VMEM] * 3,
        out_specs=(VMEM,) * 3,
        scratch_shapes=[pltpu.VMEM((3, rows, LANES), F32), pltpu.VMEM((rows, LANES), F32)],
        cost_estimate=pl.CostEstimate(flops=4 * taps * rows * columns, bytes_accessed=2 * rows * (columns + chans), transcendentals=0),
        compiler_params=params(),
        name="inner",
    )(projected, upstream, filters)


def call_rim(projected, upstream, filters, before, after, sums):
    chans = upstream.shape[1]
    groups = chans // LANES
    return pl.pallas_call(
        rim_kernel,
        out_shape=(
            jax.ShapeDtypeStruct((groups, RIM, LANES), F32),
            jax.ShapeDtypeStruct((3, groups, RIM, LANES), F32),
            jax.ShapeDtypeStruct((3, groups, RIM, LANES), F32),
            jax.ShapeDtypeStruct((2, 3 * SUB, chans // 2), F32),
        ),
        in_specs=[VMEM] * 6,
        out_specs=(VMEM,) * 4,
        scratch_shapes=[pltpu.VMEM((3, 6 * RIM, LANES), F32)],
        compiler_params=params(),
        name="rim",
    )(projected, upstream, filters, before, after, sums)


def call_back(filters, gated, grads, gated_head, head, following):
    taps = filters.shape[1]
    groups, rows, _ = gated.shape
    chans = groups * LANES
    return pl.pallas_call(
        back_kernel,
        out_shape=(jax.ShapeDtypeStruct((rows, chans), BF), jax.ShapeDtypeStruct((rows, 3 * chans), BF)),
        in_specs=[VMEM] * 6,
        out_specs=(VMEM,) * 2,
        scratch_shapes=[pltpu.VMEM((3, 4 * RIM, LANES), F32)],
        cost_estimate=pl.CostEstimate(flops=6 * taps * rows * chans, bytes_accessed=8 * rows * chans, transcendentals=0),
        compiler_params=params(),
        name="back",
    )(filters, gated, grads, gated_head, head, following)

def rounds(bits):
    return [[(1 << b) ^ 1] for b in reversed(range(3, bits))] + [[m for m in (3, 5, 6) if m < 1 << bits]]


def pack_kernel(head, tail, u_head, near, far):
    columns = head.shape[1]
    forward_near = lax.rem(lax.axis_index("seq"), 2) == 0

    first = head[...].astype(F32)[:RIM]
    last = tail[...].astype(F32)[16 - RIM :]
    near[:, :columns] = jnp.where(forward_near, last, first).astype(BF)
    far[:, :columns] = jnp.where(forward_near, first, last).astype(BF)
    cotangent = u_head[...].astype(F32)[:RIM].astype(BF)
    near[:, columns:] = cotangent
    far[:, columns:] = cotangent


def call_pack(projected, upstream):
    rows, columns = projected.shape
    chans = upstream.shape[1]
    shape = jax.ShapeDtypeStruct((RIM, columns + chans), BF)
    return pl.pallas_call(
        pack_kernel,
        grid=(1,),
        out_shape=(shape, shape),
        in_specs=[
            pl.BlockSpec((16, columns), lambda _: (0, 0)),
            pl.BlockSpec((16, columns), lambda _: (rows // 16 - 1, 0)),
            pl.BlockSpec((16, chans), lambda _: (0, 0)),
        ],
        out_specs=(VMEM,) * 2,
        name="pack",
    )(projected, projected, upstream)


def swap(array, partner):
    ways = lax.axis_size("seq")
    return lax.ppermute(array, "seq", [(i, partner(i)) for i in range(ways)])


def rims(projected, upstream):
    columns = projected.shape[1]
    ways = lax.axis_size("seq")
    me = lax.axis_index("seq")
    even = me % 2 == 0
    near, far = call_pack(projected, upstream)
    far = swap(far, lambda i: ways - 1 - i if i in (0, ways - 1) else ((i + 1) ^ 1) - 1)
    near = swap(near, lambda i: i ^ 1)
    before = jnp.where(even, far, near)[:, :columns]
    after = jnp.where(even, near, far)
    before = jnp.where(me == 0, jnp.zeros_like(before), before)
    after = jnp.where(me == ways - 1, jnp.zeros_like(after), after)
    return before, after


def shards(projected, filters, upstream):
    rows, columns = projected.shape
    ways = lax.axis_size("seq")
    me = lax.axis_index("seq")
    taps = filters.shape[1]
    chans = columns // 3
    before, after = rims(projected, upstream)
    gated, grads, sums = call_inner(projected, upstream, filters)
    *edges, halves = call_rim(projected, upstream, filters, before, after, sums)
    bits = ways.bit_length() - 1
    odd = sum((me >> b) & 1 for b in range(bits)) % 2 == 1
    mine = jnp.where(odd, halves[1], halves[0])
    mine = mine + swap(jnp.where(odd, halves[0], halves[1]), lambda i: i ^ 1)
    for step, masks in enumerate(rounds(bits)):
        sent = mine.astype(BF)
        if step == 0:
            sent, grads = lax.optimization_barrier((sent, grads))
        got = [swap(sent, lambda i: i ^ m) for m in masks]
        if step == 0:
            gated, grad_projected = call_back(filters, gated, grads, *edges)
            got, gated, grad_projected = lax.optimization_barrier((got, gated, grad_projected))
        terms = [sent.astype(F32)] + [g.astype(F32) for g in got]
        while len(terms) > 1:
            terms = [sum(terms[k : k + 2]) for k in range(0, len(terms), 2)]
        mine = terms[0]
    other = swap(mine, lambda i: i ^ 1)
    total = jnp.concatenate([jnp.where(odd, other, mine), jnp.where(odd, mine, other)], 1)
    total = total.reshape(3, SUB, chans)[:, :taps] * float(rows * ways) ** -0.5
    return gated, grad_projected, total


def solution(mesh):
    placed = (P(("groups", "seq"), None), P(), P(("groups", "seq"), None))
    return jax.shard_map(
        shards,
        mesh=mesh,
        in_specs=placed,
        out_specs=(P(("groups", "seq"), None), P(("groups", "seq"), None), P("groups", None, None)),
        check_vma=False,
    )
```

```python
import jax
import jax.numpy as jnp
from jax import lax
from jax.experimental import pallas as pl
from jax.experimental.pallas import tpu as pltpu
from jax.sharding import PartitionSpec as P

F32 = jnp.float32
BF = jnp.bfloat16
LANES = 128
SUB = 8
RIM = 8
VMEM = pl.BlockSpec(memory_space=pltpu.VMEM)
UNROLL = 4


def lanes_at(start):
    return pl.ds(pl.multiple_of(start, LANES), LANES)


def tap_rows(filters, s, n):
    return [
        jnp.broadcast_to(filters[s, j : j + 1, lanes_at(n * LANES)], (SUB, LANES))
        for j in range(filters.shape[1])
    ]


def convolve(tap, slab, s, start):
    return sum(tap[s][j] * slab[s, start - j : start - j + SUB, :] for j in range(len(tap[s])))


def gates(query, key, value, cotangent):
    product = key * value
    scaled = cotangent * query
    grads = (cotangent * product, scaled * value, scaled * key)
    return query * product, [g.astype(BF).astype(F32) for g in grads]


def inner_kernel(p_ref, u_ref, filters, gated, grads, sums, p_slab, u_slab):
    rows, columns = p_ref.shape
    chans = columns // 3
    taps = filters.shape[1]

    def group(n, carry):
        for s in range(3):
            p_slab[s] = p_ref[:, lanes_at(s * chans + n * LANES)].astype(F32)
        u_slab[...] = u_ref[:, lanes_at(n * LANES)].astype(F32)
        tap = [tap_rows(filters, s, n) for s in range(3)]
        for r in range(RIM, rows, SUB):
            conv = [convolve(tap, p_slab, s, r) for s in range(3)]
            product, grad = gates(*conv, u_slab[r : r + SUB, :])
            gated[n, r : r + SUB, :] = product
            for s in range(3):
                grads[s, n, r : r + SUB, :] = grad[s]
        for s in range(3):
            acc = [None] * taps
            for r in range(RIM, rows, SUB):
                grad = grads[s, n, r : r + SUB, :]
                for j in range(taps):
                    term = grad * p_slab[s, r - j : r - j + SUB, :]
                    acc[j] = term if r == RIM else acc[j] + term
            for j in range(taps):
                sums[n, s, j] = acc[j]
        return carry

    lax.fori_loop(0, chans // LANES, group, 0, unroll=UNROLL)


def fold(arrays):
    sub = lax.broadcasted_iota(jnp.int32, (SUB, LANES), 0)
    arrays = arrays + [jnp.zeros((SUB, LANES), F32)] * (SUB - len(arrays))
    step = 1
    while step < SUB:
        low = (sub & step) == 0
        arrays = [
            jnp.where(low, a, b) + pltpu.roll(jnp.where(low, b, a), SUB - step, 0)
            for a, b in zip(arrays[::2], arrays[1::2])
        ]
        step *= 2
    return arrays[0]


def rim_kernel(p_ref, u_ref, filters, before, after, sums, gated, head, following, totals, slab):
    rows, columns = p_ref.shape
    chans = columns // 3
    taps = filters.shape[1]
    half = chans // 2 // LANES

    def group(n, carry):
        for s in range(3):
            c = lanes_at(s * chans + n * LANES)
            slab[s, 0:RIM, :] = before[:, c].astype(F32)
            slab[s, RIM : RIM + 16, :] = p_ref[0:16, c].astype(F32)
            slab[s, RIM + 16 : RIM + 32, :] = p_ref[rows - 16 : rows, c].astype(F32)
            slab[s, RIM + 32 : RIM + 40, :] = after[:, c].astype(F32)
        tap = [tap_rows(filters, s, n) for s in range(3)]
        conv = [convolve(tap, slab, s, RIM + 32) for s in range(3)]
        _, grad = gates(*conv, after[:, lanes_at(columns + n * LANES)].astype(F32))
        for s in range(3):
            following[s, n] = grad[s]
        conv = [convolve(tap, slab, s, RIM) for s in range(3)]
        product, grad = gates(*conv, u_ref[0:16, lanes_at(n * LANES)].astype(F32)[0:RIM])
        gated[n] = product
        c = lanes_at(lax.rem(n, half) * LANES)
        for s in range(3):
            head[s, n] = grad[s]
            acc = [sums[n, s, j] + grad[s] * slab[s, RIM - j : RIM - j + SUB, :] for j in range(taps)]
            totals[n // half, s * SUB : s * SUB + SUB, c] = fold(acc)
        return carry

    lax.fori_loop(0, chans // LANES, group, 0, unroll=UNROLL)


def back_kernel(filters, gated_in, grads, gated_head, head, following, gated, out, slab, gated_slab, out_slab, sems):
    rows, columns = out.shape
    chans = columns // 3
    taps = filters.shape[1]

    def round_gated(n, carry):
        c = lanes_at(n * LANES)
        gated_slab[0:16, c] = jnp.concatenate([gated_head[n], gated_in[n, RIM:16, :]], 0).astype(BF)
        gated_slab[16:rows, c] = gated_in[n, 16:rows, :].astype(BF)
        return carry

    copies = [pltpu.make_async_copy(gated_slab, gated, sems.at[3])]
    for s in range(3):
        copies.append(pltpu.make_async_copy(out_slab.at[s], out.at[:, s * chans : (s + 1) * chans], sems.at[s]))

    lax.fori_loop(0, chans // LANES, round_gated, 0, unroll=UNROLL)
    copies[0].start()
    for s in range(3):

        def group(n, carry, s=s):
            tap = tap_rows(filters, s, n)
            slab[s, 0:RIM, :] = head[s, n]
            slab[s, RIM : 2 * RIM, :] = grads[s, n, RIM : 2 * RIM, :]
            slab[s, 2 * RIM : 3 * RIM, :] = grads[s, n, rows - RIM : rows, :]
            slab[s, 3 * RIM : 4 * RIM, :] = following[s, n]
            result = []
            for r in range(0, rows, SUB):
                if r == 0:
                    terms = [tap[j] * slab[s, j : j + SUB, :] for j in range(taps)]
                elif r == rows - SUB:
                    terms = [tap[j] * slab[s, 2 * RIM + j : 2 * RIM + j + SUB, :] for j in range(taps)]
                else:
                    terms = [tap[j] * grads[s, n, r + j : r + j + SUB, :] for j in range(taps)]
                result.append(sum(terms))
                if r % 16 == SUB:
                    out_slab[s, r - SUB : r + SUB, lanes_at(n * LANES)] = jnp.concatenate(result, 0).astype(BF)
                    result = []
            return carry

        lax.fori_loop(0, chans // LANES, group, 0, unroll=UNROLL)
        copies[s + 1].start()
    for copy in copies:
        copy.wait()


def params(**kw):
    return pltpu.CompilerParams(vmem_limit_bytes=28 * 2**20, **kw)


def call_inner(projected, upstream, filters):
    rows, columns = projected.shape
    chans = columns // 3
    groups = chans // LANES
    taps = filters.shape[1]
    return pl.pallas_call(
        inner_kernel,
        out_shape=(
            jax.ShapeDtypeStruct((groups, rows, LANES), F32),
            jax.ShapeDtypeStruct((3, groups, rows, LANES), F32),
            jax.ShapeDtypeStruct((groups, 3, taps, SUB, LANES), F32),
        ),
        in_specs=[VMEM] * 3,
        out_specs=(VMEM,) * 3,
        scratch_shapes=[pltpu.VMEM((3, rows, LANES), F32), pltpu.VMEM((rows, LANES), F32)],
        cost_estimate=pl.CostEstimate(flops=4 * taps * rows * columns, bytes_accessed=2 * rows * (columns + chans), transcendentals=0),
        compiler_params=params(),
        name="inner",
    )(projected, upstream, filters)


def call_rim(projected, upstream, filters, before, after, sums):
    chans = upstream.shape[1]
    groups = chans // LANES
    return pl.pallas_call(
        rim_kernel,
        out_shape=(
            jax.ShapeDtypeStruct((groups, RIM, LANES), F32),
            jax.ShapeDtypeStruct((3, groups, RIM, LANES), F32),
            jax.ShapeDtypeStruct((3, groups, RIM, LANES), F32),
            jax.ShapeDtypeStruct((2, 3 * SUB, chans // 2), F32),
        ),
        in_specs=[VMEM] * 6,
        out_specs=(VMEM,) * 4,
        scratch_shapes=[pltpu.VMEM((3, 6 * RIM, LANES), F32)],
        compiler_params=params(),
        name="rim",
    )(projected, upstream, filters, before, after, sums)


def call_back(filters, gated, grads, gated_head, head, following):
    taps = filters.shape[1]
    groups, rows, _ = gated.shape
    chans = groups * LANES
    return pl.pallas_call(
        back_kernel,
        out_shape=(jax.ShapeDtypeStruct((rows, chans), BF), jax.ShapeDtypeStruct((rows, 3 * chans), BF)),
        in_specs=[VMEM] * 6,
        out_specs=(pl.BlockSpec(memory_space=pltpu.HBM),) * 2,
        scratch_shapes=[
            pltpu.VMEM((3, 4 * RIM, LANES), F32),
            pltpu.VMEM((rows, chans), BF),
            pltpu.VMEM((3, rows, chans), BF),
            pltpu.SemaphoreType.DMA((4,)),
        ],
        cost_estimate=pl.CostEstimate(flops=6 * taps * rows * chans, bytes_accessed=8 * rows * chans, transcendentals=0),
        compiler_params=params(),
        name="back",
    )(filters, gated, grads, gated_head, head, following)

def rounds(bits):
    return [[(1 << b) ^ 1] for b in reversed(range(3, bits))] + [[m for m in (3, 5, 6) if m < 1 << bits]]


def pack_kernel(p_ref, u_ref, u_out, near, far, ends, sems):
    rows, columns = p_ref.shape
    copies = [
        pltpu.make_async_copy(p_ref.at[0:16], ends.at[0:16], sems.at[0]),
        pltpu.make_async_copy(p_ref.at[rows - 16 : rows], ends.at[16:32], sems.at[1]),
        pltpu.make_async_copy(u_ref, u_out, sems.at[2]),
    ]
    for copy in copies:
        copy.start()
    for copy in copies:
        copy.wait()
    forward_near = lax.rem(lax.axis_index("seq"), 2) == 0
    first = ends[0:16, :].astype(F32)[:RIM]
    last = ends[16:32, :].astype(F32)[16 - RIM :]
    near[:, :columns] = jnp.where(forward_near, last, first).astype(BF)
    far[:, :columns] = jnp.where(forward_near, first, last).astype(BF)
    cotangent = u_out[0:16, :].astype(F32)[:RIM].astype(BF)
    near[:, columns:] = cotangent
    far[:, columns:] = cotangent


def call_pack(projected, upstream):
    columns, chans = projected.shape[1], upstream.shape[1]
    shape = jax.ShapeDtypeStruct((RIM, columns + chans), BF)
    return pl.pallas_call(
        pack_kernel,
        out_shape=(jax.ShapeDtypeStruct(upstream.shape, BF), shape, shape),
        in_specs=[pl.BlockSpec(memory_space=pltpu.HBM)] * 2,
        out_specs=(VMEM,) * 3,
        scratch_shapes=[pltpu.VMEM((32, columns), BF), pltpu.SemaphoreType.DMA((3,))],
        compiler_params=params(),
        name="pack",
    )(*[pltpu.with_memory_space_constraint(a, pltpu.HBM) for a in (projected, upstream)])


def swap(array, partner):
    ways = lax.axis_size("seq")
    return lax.ppermute(array, "seq", [(i, partner(i)) for i in range(ways)])


def trade_far(array):
    groups, ways = lax.axis_size("groups"), lax.axis_size("seq")

    def partner(g, i):
        if i not in (0, ways - 1):
            return g, ((i + 1) ^ 1) - 1
        return (g ^ 1, i) if groups % 2 == 0 else (g, ways - 1 - i)

    places = [(g, i) for g in range(groups) for i in range(ways)]
    pairs = [(g * ways + i, partner(g, i)[0] * ways + partner(g, i)[1]) for g, i in places]
    return lax.ppermute(array, ("groups", "seq"), pairs)


def rims(projected, upstream):
    columns = projected.shape[1]
    ways = lax.axis_size("seq")
    me = lax.axis_index("seq")
    even = me % 2 == 0
    upstream, near, far = call_pack(projected, upstream)
    far = trade_far(far)
    near = swap(near, lambda i: i ^ 1)
    before = jnp.where(even, far, near)[:, :columns]
    after = jnp.where(even, near, far)
    before = jnp.where(me == 0, jnp.zeros_like(before), before)
    after = jnp.where(me == ways - 1, jnp.zeros_like(after), after)
    return upstream, before, after


def shards(projected, filters, upstream):
    rows, columns = projected.shape
    ways = lax.axis_size("seq")
    me = lax.axis_index("seq")
    taps = filters.shape[1]
    chans = columns // 3
    upstream, before, after = rims(projected, upstream)
    gated, grads, sums = call_inner(projected, upstream, filters)
    *edges, halves = call_rim(projected, upstream, filters, before, after, sums)
    bits = ways.bit_length() - 1
    odd = sum((me >> b) & 1 for b in range(bits)) % 2 == 1
    mine = jnp.where(odd, halves[1], halves[0])
    mine = mine + swap(jnp.where(odd, halves[0], halves[1]), lambda i: i ^ 1)
    for step, masks in enumerate(rounds(bits)):
        sent = mine.astype(BF)
        if step == len(rounds(bits)) - 1:
            sent, grads = lax.optimization_barrier((sent, grads))
        got = [swap(sent, lambda i: i ^ m) for m in masks]
        if step == len(rounds(bits)) - 1:
            gated, grad_projected = call_back(filters, gated, grads, *edges)
            got, gated, grad_projected = lax.optimization_barrier((got, gated, grad_projected))
        terms = [sent.astype(F32)] + [g.astype(F32) for g in got]
        while len(terms) > 1:
            terms = [sum(terms[k : k + 2]) for k in range(0, len(terms), 2)]
        mine = terms[0]
    other = swap(mine, lambda i: i ^ 1)
    total = jnp.concatenate([jnp.where(odd, other, mine), jnp.where(odd, mine, other)], 1)
    total = total.reshape(3, SUB, chans)[:, :taps] * float(rows * ways) ** -0.5
    return gated, grad_projected, total


def solution(mesh):
    placed = (P(("groups", "seq"), None), P(), P(("groups", "seq"), None))
    return jax.shard_map(
        shards,
        mesh=mesh,
        in_specs=placed,
        out_specs=(P(("groups", "seq"), None), P(("groups", "seq"), None), P("groups", None, None)),
        check_vma=False,
    )
```

```python
import functools

import jax
import jax.numpy as jnp
from jax import lax
from jax.experimental import pallas as pl
from jax.experimental.pallas import tpu as pltpu
from jax.sharding import PartitionSpec as P

F32 = jnp.float32
BF = jnp.bfloat16
LANES = 128
SUB = 8
RIM = 8
REACH = 6
VMEM = pl.BlockSpec(memory_space=pltpu.VMEM)
UNROLL = 4


def lanes_at(start):
    return pl.ds(pl.multiple_of(start, LANES), LANES)


def tap_rows(filters, s, n):
    return [
        jnp.broadcast_to(filters[s, j : j + 1, lanes_at(n * LANES)], (SUB, LANES))
        for j in range(filters.shape[1])
    ]


def convolve(tap, slab, s, start):
    return sum(tap[s][j] * slab[s, start - j : start - j + SUB, :] for j in range(len(tap[s])))


def gates(query, key, value, cotangent):
    product = key * value
    scaled = cotangent * query
    grads = (cotangent * product, scaled * value, scaled * key)
    return query * product, [g.astype(BF).astype(F32) for g in grads]


def inner_kernel(p_ref, u_ref, filters, gated, grads, sums, p_slab, u_slab):
    rows, columns = p_ref.shape
    chans = columns // 3
    taps = filters.shape[1]

    def group(n, carry):
        for s in range(3):
            p_slab[s] = p_ref[:, lanes_at(s * chans + n * LANES)].astype(F32)
        u_slab[...] = u_ref[:, lanes_at(n * LANES)].astype(F32)
        tap = [tap_rows(filters, s, n) for s in range(3)]
        for r in range(RIM, rows, SUB):
            conv = [convolve(tap, p_slab, s, r) for s in range(3)]
            product, grad = gates(*conv, u_slab[r : r + SUB, :])
            gated[n, r : r + SUB, :] = product
            for s in range(3):
                grads[s, n, r : r + SUB, :] = grad[s]
        for s in range(3):
            acc = [None] * taps
            for r in range(RIM, rows, SUB):
                grad = grads[s, n, r : r + SUB, :]
                for j in range(taps):
                    term = grad * p_slab[s, r - j : r - j + SUB, :]
                    acc[j] = term if r == RIM else acc[j] + term
            for j in range(taps):
                sums[n, s, j] = acc[j]
        return carry

    lax.fori_loop(0, chans // LANES, group, 0, unroll=UNROLL)


def fold(arrays):
    sub = lax.broadcasted_iota(jnp.int32, (SUB, LANES), 0)
    arrays = arrays + [jnp.zeros((SUB, LANES), F32)] * (SUB - len(arrays))
    step = 1
    while step < SUB:
        low = (sub & step) == 0
        arrays = [
            jnp.where(low, a, b) + pltpu.roll(jnp.where(low, b, a), SUB - step, 0)
            for a, b in zip(arrays[::2], arrays[1::2])
        ]
        step *= 2
    return arrays[0]


def rim_kernel(p_ref, u_ref, filters, before, sums, gated, head, totals, slab):
    rows, columns = p_ref.shape
    chans = columns // 3
    taps = filters.shape[1]
    half = chans // 2 // LANES

    def group(n, carry):
        for s in range(3):
            c = lanes_at(s * chans + n * LANES)
            slab[s, 0:RIM, :] = pltpu.roll(before[:, c].astype(F32), RIM - REACH, 0)
            slab[s, RIM : RIM + 16, :] = p_ref[0:16, c].astype(F32)
        tap = [tap_rows(filters, s, n) for s in range(3)]
        conv = [convolve(tap, slab, s, RIM) for s in range(3)]
        product, grad = gates(*conv, u_ref[0:16, lanes_at(n * LANES)].astype(F32)[0:RIM])
        gated[n] = product
        for s in range(3):
            head[s, n] = grad[s]
            acc = [sums[n, s, j] + grad[s] * slab[s, RIM - j : RIM - j + SUB, :] for j in range(taps)]
            place = pl.ds(s * taps * half + lax.rem(n, half), taps, stride=half)
            totals[n // half, place, :] = fold(acc)[:taps]
        return carry

    lax.fori_loop(0, chans // LANES, group, 0, unroll=UNROLL)


def next_kernel(p_ref, filters, after, following, slab):
    rows, columns = p_ref.shape
    chans = columns // 3
    sub = lax.broadcasted_iota(jnp.int32, (SUB, LANES), 0)

    def group(n, carry):
        cotangent = jnp.zeros((SUB, LANES), F32)
        for s in range(3):
            c = lanes_at(s * chans + n * LANES)
            tile = after[:, c].astype(F32)
            slab[s, 0:16, :] = p_ref[rows - 16 : rows, c].astype(F32)
            slab[s, 16 : 16 + RIM, :] = tile
            cotangent = jnp.where(sub == s, pltpu.roll(tile, s + 2, 0), cotangent)
            cotangent = jnp.where(sub == s + 3, pltpu.roll(tile, s + 4, 0), cotangent)
        tap = [tap_rows(filters, s, n) for s in range(3)]
        conv = [convolve(tap, slab, s, 16) for s in range(3)]
        _, grad = gates(*conv, cotangent)
        for s in range(3):
            following[s, n] = grad[s]
        return carry

    lax.fori_loop(0, chans // LANES, group, 0, unroll=UNROLL)


def back_kernel(filters, gated_in, grads, gated_head, head, following, gated, out, slab, gated_slab, out_slab, sems):
    rows, columns = out.shape
    chans = columns // 3
    taps = filters.shape[1]

    def round_gated(n, carry):
        c = lanes_at(n * LANES)
        gated_slab[0:16, c] = jnp.concatenate([gated_head[n], gated_in[n, RIM:16, :]], 0).astype(BF)
        gated_slab[16:rows, c] = gated_in[n, 16:rows, :].astype(BF)
        return carry

    copies = [pltpu.make_async_copy(gated_slab, gated, sems.at[3])]
    for s in range(3):
        copies.append(pltpu.make_async_copy(out_slab.at[s], out.at[:, s * chans : (s + 1) * chans], sems.at[s]))

    lax.fori_loop(0, chans // LANES, round_gated, 0, unroll=UNROLL)
    copies[0].start()
    for s in range(3):

        def group(n, carry, s=s):
            tap = tap_rows(filters, s, n)
            slab[s, 0:RIM, :] = head[s, n]
            slab[s, RIM : 2 * RIM, :] = grads[s, n, RIM : 2 * RIM, :]
            slab[s, 2 * RIM : 3 * RIM, :] = grads[s, n, rows - RIM : rows, :]
            slab[s, 3 * RIM : 4 * RIM, :] = following[s, n]
            result = []
            for r in range(0, rows, SUB):
                if r == 0:
                    terms = [tap[j] * slab[s, j : j + SUB, :] for j in range(taps)]
                elif r == rows - SUB:
                    terms = [tap[j] * slab[s, 2 * RIM + j : 2 * RIM + j + SUB, :] for j in range(taps)]
                else:
                    terms = [tap[j] * grads[s, n, r + j : r + j + SUB, :] for j in range(taps)]
                result.append(sum(terms))
                if r % 16 == SUB:
                    out_slab[s, r - SUB : r + SUB, lanes_at(n * LANES)] = jnp.concatenate(result, 0).astype(BF)
                    result = []
            return carry

        lax.fori_loop(0, chans // LANES, group, 0, unroll=UNROLL)
        copies[s + 1].start()
    for copy in copies:
        copy.wait()


def params(**kw):
    return pltpu.CompilerParams(vmem_limit_bytes=28 * 2**20, **kw)


def call_inner(projected, upstream, filters):
    rows, columns = projected.shape
    chans = columns // 3
    groups = chans // LANES
    taps = filters.shape[1]
    return pl.pallas_call(
        inner_kernel,
        out_shape=(
            jax.ShapeDtypeStruct((groups, rows, LANES), F32),
            jax.ShapeDtypeStruct((3, groups, rows, LANES), F32),
            jax.ShapeDtypeStruct((groups, 3, taps, SUB, LANES), F32),
        ),
        in_specs=[VMEM] * 3,
        out_specs=(VMEM,) * 3,
        scratch_shapes=[pltpu.VMEM((3, rows, LANES), F32), pltpu.VMEM((rows, LANES), F32)],
        cost_estimate=pl.CostEstimate(flops=4 * taps * rows * columns, bytes_accessed=2 * rows * (columns + chans), transcendentals=0),
        compiler_params=params(),
        name="inner",
    )(projected, upstream, filters)


def call_rim(projected, upstream, filters, before, sums):
    chans = upstream.shape[1]
    groups = chans // LANES
    taps = filters.shape[1]
    return pl.pallas_call(
        rim_kernel,
        out_shape=(
            jax.ShapeDtypeStruct((groups, RIM, LANES), F32),
            jax.ShapeDtypeStruct((3, groups, RIM, LANES), F32),
            jax.ShapeDtypeStruct((2, 3 * taps * groups // 2, LANES), F32),
        ),
        in_specs=[VMEM] * 5,
        out_specs=(VMEM,) * 3,
        scratch_shapes=[pltpu.VMEM((3, RIM + 16, LANES), F32)],
        compiler_params=params(),
        name="rim",
    )(projected, upstream, filters, before, sums)


def call_next(projected, filters, after):
    groups = filters.shape[2] // LANES
    return pl.pallas_call(
        next_kernel,
        out_shape=jax.ShapeDtypeStruct((3, groups, RIM, LANES), F32),
        in_specs=[VMEM] * 3,
        out_specs=VMEM,
        scratch_shapes=[pltpu.VMEM((3, 16 + RIM, LANES), F32)],
        compiler_params=params(),
        name="next",
    )(projected, filters, after)


def place_kernel(scale, bits, mine, other, out):
    _, taps, chans = out.shape
    half = chans // 2 // LANES
    me = lax.axis_index("seq")
    odd = lax.rem(sum(lax.rem(me // 2**b, 2) for b in range(bits)), 2)
    for s in range(3):
        for n in range(half):
            place = pl.ds(s * taps * half + n, taps, stride=half)
            out[s, :, lanes_at((odd * half + n) * LANES)] = mine[place, :] * scale
            out[s, :, lanes_at(((1 - odd) * half + n) * LANES)] = other[place, :] * scale


def call_place(mine, other, scale, bits, shape):
    return pl.pallas_call(
        functools.partial(place_kernel, scale, bits),
        out_shape=jax.ShapeDtypeStruct(shape, F32),
        in_specs=[VMEM] * 2,
        out_specs=VMEM,
        compiler_params=params(),
        name="place",
    )(mine, other)


def call_back(filters, gated, grads, gated_head, head, following):
    taps = filters.shape[1]
    groups, rows, _ = gated.shape
    chans = groups * LANES
    return pl.pallas_call(
        back_kernel,
        out_shape=(jax.ShapeDtypeStruct((rows, chans), BF), jax.ShapeDtypeStruct((rows, 3 * chans), BF)),
        in_specs=[VMEM] * 6,
        out_specs=(pl.BlockSpec(memory_space=pltpu.HBM),) * 2,
        scratch_shapes=[
            pltpu.VMEM((3, 4 * RIM, LANES), F32),
            pltpu.VMEM((rows, chans), BF),
            pltpu.VMEM((3, rows, chans), BF),
            pltpu.SemaphoreType.DMA((4,)),
        ],
        cost_estimate=pl.CostEstimate(flops=6 * taps * rows * chans, bytes_accessed=8 * rows * chans, transcendentals=0),
        compiler_params=params(),
        name="back",
    )(filters, gated, grads, gated_head, head, following)

def rounds(bits):
    return [[(1 << b) ^ 1] for b in reversed(range(3, bits))] + [[m for m in (3, 5, 6) if m < 1 << bits]]


def pack_kernel(p_ref, u_ref, u_out, near, far, ends, sems):
    rows, columns = p_ref.shape
    copies = [
        pltpu.make_async_copy(p_ref.at[0:16], ends.at[0:16], sems.at[0]),
        pltpu.make_async_copy(p_ref.at[rows - 16 : rows], ends.at[16:32], sems.at[1]),
        pltpu.make_async_copy(u_ref, u_out, sems.at[2]),
    ]
    for copy in copies:
        copy.start()
    for copy in copies:
        copy.wait()
    forward_near = lax.rem(lax.axis_index("seq"), 2) == 0
    chans = columns // 3
    sub = lax.broadcasted_iota(jnp.int32, (SUB, LANES), 0)

    def group(n, carry):
        cotangent = u_out[0:16, lanes_at(n * LANES)].astype(F32)[:RIM]
        for s in range(3):
            c = lanes_at(s * chans + n * LANES)
            last = pltpu.roll(ends[16:32, c].astype(F32)[16 - RIM :], REACH, 0)
            first = ends[0:16, c].astype(F32)[:RIM]
            first = jnp.where(sub == 6, pltpu.roll(cotangent, 6 - s, 0), first)
            first = jnp.where(sub == 7, pltpu.roll(cotangent, 4 - s, 0), first)
            near[:, c] = jnp.where(forward_near, last, first).astype(BF)
            far[:, c] = jnp.where(forward_near, first, last).astype(BF)
        return carry

    lax.fori_loop(0, chans // LANES, group, 0, unroll=UNROLL)


def call_pack(projected, upstream):
    columns = projected.shape[1]
    shape = jax.ShapeDtypeStruct((RIM, columns), BF)
    return pl.pallas_call(
        pack_kernel,
        out_shape=(jax.ShapeDtypeStruct(upstream.shape, BF), shape, shape),
        in_specs=[pl.BlockSpec(memory_space=pltpu.HBM)] * 2,
        out_specs=(VMEM,) * 3,
        scratch_shapes=[pltpu.VMEM((32, columns), BF), pltpu.SemaphoreType.DMA((3,))],
        compiler_params=params(),
        name="pack",
    )(*[pltpu.with_memory_space_constraint(a, pltpu.HBM) for a in (projected, upstream)])


def swap(array, partner):
    ways = lax.axis_size("seq")
    return lax.ppermute(array, "seq", [(i, partner(i)) for i in range(ways)])


def trade_far(array):
    groups, ways = lax.axis_size("groups"), lax.axis_size("seq")

    def partner(g, i):
        if i not in (0, ways - 1):
            return g, ((i + 1) ^ 1) - 1
        return (g ^ 1, i) if groups % 2 == 0 else (g, ways - 1 - i)

    places = [(g, i) for g in range(groups) for i in range(ways)]
    pairs = [(g * ways + i, partner(g, i)[0] * ways + partner(g, i)[1]) for g, i in places]
    return lax.ppermute(array, ("groups", "seq"), pairs)


def rims(projected, upstream):
    ways = lax.axis_size("seq")
    me = lax.axis_index("seq")
    even = me % 2 == 0
    upstream, near, far = call_pack(projected, upstream)
    far = trade_far(far)
    near = swap(near, lambda i: i ^ 1)
    before = jnp.where(even, far, near)
    after = jnp.where(even, near, far)
    before = jnp.where(me == 0, jnp.zeros_like(before), before)
    after = jnp.where(me == ways - 1, jnp.zeros_like(after), after)
    return upstream, before, after


def shards(projected, filters, upstream):
    rows = projected.shape[0]
    ways = lax.axis_size("seq")
    me = lax.axis_index("seq")
    upstream, before, after = rims(projected, upstream)
    gated, grads, sums = call_inner(projected, upstream, filters)
    gated_head, head, halves = call_rim(projected, upstream, filters, before, sums)
    bits = ways.bit_length() - 1
    odd = sum((me >> b) & 1 for b in range(bits)) % 2 == 1
    mine = jnp.where(odd, halves[1], halves[0])
    mine = mine + swap(jnp.where(odd, halves[0], halves[1]), lambda i: i ^ 1)
    steps = rounds(bits)
    for step, masks in enumerate(steps):
        sent = mine.astype(BF)
        if step == 0:
            sent, after = lax.optimization_barrier((sent, after))
        if step == len(steps) - 1:
            sent, grads = lax.optimization_barrier((sent, grads))
        got = [swap(sent, lambda i: i ^ m) for m in masks]
        if step == 0:
            following = call_next(projected, filters, after)
            got, following = lax.optimization_barrier((got, following))
        if step == len(steps) - 1:
            gated, grad_projected = call_back(filters, gated, grads, gated_head, head, following)
            got, gated, grad_projected = lax.optimization_barrier((got, gated, grad_projected))
        terms = [sent.astype(F32)] + [g.astype(F32) for g in got]
        while len(terms) > 1:
            terms = [sum(terms[k : k + 2]) for k in range(0, len(terms), 2)]
        mine = terms[0]
    other = swap(mine, lambda i: i ^ 1)
    total = call_place(mine, other, float(rows * ways) ** -0.5, bits, filters.shape)
    return gated, grad_projected, total


def solution(mesh):
    placed = (P(("groups", "seq"), None), P(), P(("groups", "seq"), None))
    return jax.shard_map(
        shards,
        mesh=mesh,
        in_specs=placed,
        out_specs=(P(("groups", "seq"), None), P(("groups", "seq"), None), P("groups", None, None)),
        check_vma=False,
    )
```

```python
import functools

import jax
import jax.numpy as jnp
from jax import lax
from jax.experimental import pallas as pl
from jax.experimental.pallas import tpu as pltpu
from jax.sharding import PartitionSpec as P

F32 = jnp.float32
BF = jnp.bfloat16
LANES = 128
SUB = 8
RIM = 8
REACH = 6
VMEM = pl.BlockSpec(memory_space=pltpu.VMEM)
HBM = pl.BlockSpec(memory_space=pltpu.HBM)
UNROLL = 4


def lanes_at(start):
    return pl.ds(pl.multiple_of(start, LANES), LANES)


def tap_rows(filters, s, n):
    return [
        jnp.broadcast_to(filters[s, j : j + 1, lanes_at(n * LANES)], (SUB, LANES))
        for j in range(filters.shape[1])
    ]


def convolve(tap, slab, s, n, start):
    return sum(tap[j] * slab[s, n, start - j : start - j + SUB, :] for j in range(len(tap)))


def gates(query, key, value, cotangent):
    product = key * value
    scaled = cotangent * query
    grads = (cotangent * product, scaled * value, scaled * key)
    return query * product, [g.astype(BF).astype(F32) for g in grads]


def inner_kernel(p_ref, u_hbm, filters, gated, grads, sums, p_slab, u_ref, u_slab, sem):
    rows, columns = p_ref.shape
    chans = columns // 3
    taps = filters.shape[1]
    fetch = pltpu.make_async_copy(u_hbm, u_ref, sem)
    fetch.start()

    def filter_group(n, carry):
        for s in range(3):
            p_slab[s, n] = p_ref[:, lanes_at(s * chans + n * LANES)].astype(F32)
            tap = tap_rows(filters, s, n)
            for r in range(RIM, rows, SUB):
                grads[s, n, r : r + SUB, :] = convolve(tap, p_slab, s, n, r)
        return carry

    def gate_group(n, carry):
        u_slab[...] = u_ref[:, lanes_at(n * LANES)].astype(F32)
        for r in range(RIM, rows, SUB):
            conv = [grads[s, n, r : r + SUB, :] for s in range(3)]
            product, grad = gates(*conv, u_slab[r : r + SUB, :])
            gated[n, r : r + SUB, :] = product
            for s in range(3):
                grads[s, n, r : r + SUB, :] = grad[s]
        for s in range(3):
            acc = [None] * taps
            for r in range(RIM, rows, SUB):
                grad = grads[s, n, r : r + SUB, :]
                for j in range(taps):
                    term = grad * p_slab[s, n, r - j : r - j + SUB, :]
                    acc[j] = term if r == RIM else acc[j] + term
            for j in range(taps):
                sums[n, s, j] = acc[j]
        return carry

    groups = chans // LANES
    lax.fori_loop(0, groups, filter_group, 0, unroll=UNROLL)
    fetch.wait()
    lax.fori_loop(0, groups, gate_group, 0, unroll=UNROLL)


def fold(arrays):
    sub = lax.broadcasted_iota(jnp.int32, (SUB, LANES), 0)
    arrays = arrays + [jnp.zeros((SUB, LANES), F32)] * (SUB - len(arrays))
    step = 1
    while step < SUB:
        low = (sub & step) == 0
        arrays = [
            jnp.where(low, a, b) + pltpu.roll(jnp.where(low, b, a), SUB - step, 0)
            for a, b in zip(arrays[::2], arrays[1::2])
        ]
        step *= 2
    return arrays[0]


def rim_kernel(p_ref, u_head, filters, before, sums, gated, head, totals, slab):
    rows, columns = p_ref.shape
    chans = columns // 3
    taps = filters.shape[1]
    half = chans // 2 // LANES

    def group(n, carry):
        for s in range(3):
            c = lanes_at(s * chans + n * LANES)
            slab[s, 0, 0:RIM, :] = pltpu.roll(before[:, c].astype(F32), RIM - REACH, 0)
            slab[s, 0, RIM : RIM + 16, :] = p_ref[0:16, c].astype(F32)
        conv = [convolve(tap_rows(filters, s, n), slab, s, 0, RIM) for s in range(3)]
        product, grad = gates(*conv, u_head[:, lanes_at(n * LANES)].astype(F32)[0:RIM])
        gated[n] = product
        for s in range(3):
            head[s, n] = grad[s]
            acc = [sums[n, s, j] + grad[s] * slab[s, 0, RIM - j : RIM - j + SUB, :] for j in range(taps)]
            place = pl.ds(s * taps * half + lax.rem(n, half), taps, stride=half)
            totals[n // half, place, :] = fold(acc)[:taps]
        return carry

    lax.fori_loop(0, chans // LANES, group, 0, unroll=UNROLL)


def next_kernel(p_ref, filters, after, following, slab):
    rows, columns = p_ref.shape
    chans = columns // 3
    sub = lax.broadcasted_iota(jnp.int32, (SUB, LANES), 0)

    def group(n, carry):
        cotangent = jnp.zeros((SUB, LANES), F32)
        for s in range(3):
            c = lanes_at(s * chans + n * LANES)
            tile = after[:, c].astype(F32)
            slab[s, 0, 0:16, :] = p_ref[rows - 16 : rows, c].astype(F32)
            slab[s, 0, 16 : 16 + RIM, :] = tile
            cotangent = jnp.where(sub == s, pltpu.roll(tile, s + 2, 0), cotangent)
            cotangent = jnp.where(sub == s + 3, pltpu.roll(tile, s + 4, 0), cotangent)
        conv = [convolve(tap_rows(filters, s, n), slab, s, 0, 16) for s in range(3)]
        _, grad = gates(*conv, cotangent)
        for s in range(3):
            following[s, n] = grad[s]
        return carry

    lax.fori_loop(0, chans // LANES, group, 0, unroll=UNROLL)


def back_kernel(filters, gated_in, grads, gated_head, head, following, gated, out, slab, gated_slab, out_slab, sems):
    rows, columns = out.shape
    chans = columns // 3
    taps = filters.shape[1]

    def round_gated(n, carry):
        c = lanes_at(n * LANES)
        gated_slab[0:16, c] = jnp.concatenate([gated_head[n], gated_in[n, RIM:16, :]], 0).astype(BF)
        gated_slab[16:rows, c] = gated_in[n, 16:rows, :].astype(BF)
        return carry

    copies = [pltpu.make_async_copy(gated_slab, gated, sems.at[3])]
    for s in range(3):
        copies.append(pltpu.make_async_copy(out_slab.at[s], out.at[:, s * chans : (s + 1) * chans], sems.at[s]))

    lax.fori_loop(0, chans // LANES, round_gated, 0, unroll=UNROLL)
    copies[0].start()
    for s in range(3):

        def group(n, carry, s=s):
            tap = tap_rows(filters, s, n)
            slab[s, 0:RIM, :] = head[s, n]
            slab[s, RIM : 2 * RIM, :] = grads[s, n, RIM : 2 * RIM, :]
            slab[s, 2 * RIM : 3 * RIM, :] = grads[s, n, rows - RIM : rows, :]
            slab[s, 3 * RIM : 4 * RIM, :] = following[s, n]
            result = []
            for r in range(0, rows, SUB):
                if r == 0:
                    terms = [tap[j] * slab[s, j : j + SUB, :] for j in range(taps)]
                elif r == rows - SUB:
                    terms = [tap[j] * slab[s, 2 * RIM + j : 2 * RIM + j + SUB, :] for j in range(taps)]
                else:
                    terms = [tap[j] * grads[s, n, r + j : r + j + SUB, :] for j in range(taps)]
                result.append(sum(terms))
                if r % 16 == SUB:
                    out_slab[s, r - SUB : r + SUB, lanes_at(n * LANES)] = jnp.concatenate(result, 0).astype(BF)
                    result = []
            return carry

        lax.fori_loop(0, chans // LANES, group, 0, unroll=UNROLL)
        copies[s + 1].start()
    for copy in copies:
        copy.wait()


def in_hbm(array):
    return pltpu.with_memory_space_constraint(array, pltpu.HBM)


def params(**kw):
    return pltpu.CompilerParams(vmem_limit_bytes=28 * 2**20, **kw)


def call_inner(projected, upstream, filters):
    rows, columns = projected.shape
    chans = columns // 3
    groups = chans // LANES
    taps = filters.shape[1]
    return pl.pallas_call(
        inner_kernel,
        out_shape=(
            jax.ShapeDtypeStruct((groups, rows, LANES), F32),
            jax.ShapeDtypeStruct((3, groups, rows, LANES), F32),
            jax.ShapeDtypeStruct((groups, 3, taps, SUB, LANES), F32),
        ),
        in_specs=[VMEM, HBM, VMEM],
        out_specs=(VMEM,) * 3,
        scratch_shapes=[
            pltpu.VMEM((3, groups, rows, LANES), F32),
            pltpu.VMEM((rows, chans), BF),
            pltpu.VMEM((rows, LANES), F32),
            pltpu.SemaphoreType.DMA,
        ],
        cost_estimate=pl.CostEstimate(flops=4 * taps * rows * columns, bytes_accessed=2 * rows * (columns + chans), transcendentals=0),
        compiler_params=params(),
        name="inner",
    )(projected, in_hbm(upstream), filters)


def call_rim(projected, u_head, filters, before, sums):
    chans = u_head.shape[1]
    groups = chans // LANES
    taps = filters.shape[1]
    return pl.pallas_call(
        rim_kernel,
        out_shape=(
            jax.ShapeDtypeStruct((groups, RIM, LANES), F32),
            jax.ShapeDtypeStruct((3, groups, RIM, LANES), F32),
            jax.ShapeDtypeStruct((2, 3 * taps * groups // 2, LANES), F32),
        ),
        in_specs=[VMEM] * 5,
        out_specs=(VMEM,) * 3,
        scratch_shapes=[pltpu.VMEM((3, 1, RIM + 16, LANES), F32)],
        compiler_params=params(),
        name="rim",
    )(projected, u_head, filters, before, sums)


def call_next(projected, filters, after):
    groups = filters.shape[2] // LANES
    return pl.pallas_call(
        next_kernel,
        out_shape=jax.ShapeDtypeStruct((3, groups, RIM, LANES), F32),
        in_specs=[VMEM] * 3,
        out_specs=VMEM,
        scratch_shapes=[pltpu.VMEM((3, 1, 16 + RIM, LANES), F32)],
        compiler_params=params(),
        name="next",
    )(projected, filters, after)


def place_kernel(scale, bits, mine, other, out):
    _, taps, chans = out.shape
    half = chans // 2 // LANES
    me = lax.axis_index("seq")
    odd = lax.rem(sum(lax.rem(me // 2**b, 2) for b in range(bits)), 2)
    for s in range(3):
        for n in range(half):
            place = pl.ds(s * taps * half + n, taps, stride=half)
            out[s, :, lanes_at((odd * half + n) * LANES)] = mine[place, :] * scale
            out[s, :, lanes_at(((1 - odd) * half + n) * LANES)] = other[place, :] * scale


def call_place(mine, other, scale, bits, shape):
    return pl.pallas_call(
        functools.partial(place_kernel, scale, bits),
        out_shape=jax.ShapeDtypeStruct(shape, F32),
        in_specs=[VMEM] * 2,
        out_specs=VMEM,
        compiler_params=params(),
        name="place",
    )(mine, other)


def call_back(filters, gated, grads, gated_head, head, following):
    taps = filters.shape[1]
    groups, rows, _ = gated.shape
    chans = groups * LANES
    return pl.pallas_call(
        back_kernel,
        out_shape=(jax.ShapeDtypeStruct((rows, chans), BF), jax.ShapeDtypeStruct((rows, 3 * chans), BF)),
        in_specs=[VMEM] * 6,
        out_specs=(HBM,) * 2,
        scratch_shapes=[
            pltpu.VMEM((3, 4 * RIM, LANES), F32),
            pltpu.VMEM((rows, chans), BF),
            pltpu.VMEM((3, rows, chans), BF),
            pltpu.SemaphoreType.DMA((4,)),
        ],
        cost_estimate=pl.CostEstimate(flops=6 * taps * rows * chans, bytes_accessed=8 * rows * chans, transcendentals=0),
        compiler_params=params(),
        name="back",
    )(filters, gated, grads, gated_head, head, following)

def rounds(bits):
    return [[(1 << b) ^ 1] for b in reversed(range(3, bits))] + [[m for m in (3, 5, 6) if m < 1 << bits]]


def pack_kernel(p_ref, u_ref, u_head, near, far, ends, sems):
    rows, columns = p_ref.shape
    copies = [
        pltpu.make_async_copy(p_ref.at[0:16], ends.at[0:16], sems.at[0]),
        pltpu.make_async_copy(p_ref.at[rows - 16 : rows], ends.at[16:32], sems.at[1]),
        pltpu.make_async_copy(u_ref.at[0:16], u_head, sems.at[2]),
    ]
    for copy in copies:
        copy.start()
    for copy in copies:
        copy.wait()
    forward_near = lax.rem(lax.axis_index("seq"), 2) == 0
    chans = columns // 3
    sub = lax.broadcasted_iota(jnp.int32, (SUB, LANES), 0)

    def group(n, carry):
        cotangent = u_head[:, lanes_at(n * LANES)].astype(F32)[:RIM]
        for s in range(3):
            c = lanes_at(s * chans + n * LANES)
            last = pltpu.roll(ends[16:32, c].astype(F32)[16 - RIM :], REACH, 0)
            first = ends[0:16, c].astype(F32)[:RIM]
            first = jnp.where(sub == 6, pltpu.roll(cotangent, 6 - s, 0), first)
            first = jnp.where(sub == 7, pltpu.roll(cotangent, 4 - s, 0), first)
            near[:, c] = jnp.where(forward_near, last, first).astype(BF)
            far[:, c] = jnp.where(forward_near, first, last).astype(BF)
        return carry

    lax.fori_loop(0, chans // LANES, group, 0, unroll=UNROLL)


def call_pack(projected, upstream):
    columns = projected.shape[1]
    shape = jax.ShapeDtypeStruct((RIM, columns), BF)
    return pl.pallas_call(
        pack_kernel,
        out_shape=(jax.ShapeDtypeStruct((16, upstream.shape[1]), BF), shape, shape),
        in_specs=[HBM] * 2,
        out_specs=(VMEM,) * 3,
        scratch_shapes=[pltpu.VMEM((32, columns), BF), pltpu.SemaphoreType.DMA((3,))],
        compiler_params=params(),
        name="pack",
    )(in_hbm(projected), in_hbm(upstream))


def swap(array, partner):
    ways = lax.axis_size("seq")
    return lax.ppermute(array, "seq", [(i, partner(i)) for i in range(ways)])


def trade_far(array):
    groups, ways = lax.axis_size("groups"), lax.axis_size("seq")

    def partner(g, i):
        if i not in (0, ways - 1):
            return g, ((i + 1) ^ 1) - 1
        return (g ^ 1, i) if groups % 2 == 0 else (g, ways - 1 - i)

    places = [(g, i) for g in range(groups) for i in range(ways)]
    pairs = [(g * ways + i, partner(g, i)[0] * ways + partner(g, i)[1]) for g, i in places]
    return lax.ppermute(array, ("groups", "seq"), pairs)


def rims(projected, upstream):
    ways = lax.axis_size("seq")
    me = lax.axis_index("seq")
    even = me % 2 == 0
    u_head, near, far = call_pack(projected, upstream)
    far = trade_far(far)
    near = swap(near, lambda i: i ^ 1)
    before = jnp.where(even, far, near)
    after = jnp.where(even, near, far)
    before = jnp.where(me == 0, jnp.zeros_like(before), before)
    after = jnp.where(me == ways - 1, jnp.zeros_like(after), after)
    return u_head, before, after


def shards(projected, filters, upstream):
    rows = projected.shape[0]
    ways = lax.axis_size("seq")
    me = lax.axis_index("seq")
    u_head, before, after = rims(projected, upstream)
    gated, grads, sums = call_inner(projected, upstream, filters)
    gated_head, head, halves = call_rim(projected, u_head, filters, before, sums)
    bits = ways.bit_length() - 1
    odd = sum((me >> b) & 1 for b in range(bits)) % 2 == 1
    mine = jnp.where(odd, halves[1], halves[0])
    mine = mine + swap(jnp.where(odd, halves[0], halves[1]), lambda i: i ^ 1)
    steps = rounds(bits)
    for step, masks in enumerate(steps):
        sent = mine.astype(BF)
        if step == 0:
            sent, after = lax.optimization_barrier((sent, after))
        if step == len(steps) - 1:
            sent, grads = lax.optimization_barrier((sent, grads))
        got = [swap(sent, lambda i: i ^ m) for m in masks]
        if step == 0:
            following = call_next(projected, filters, after)
            got, following = lax.optimization_barrier((got, following))
        if step == len(steps) - 1:
            gated, grad_projected = call_back(filters, gated, grads, gated_head, head, following)
            got, gated, grad_projected = lax.optimization_barrier((got, gated, grad_projected))
        terms = [sent.astype(F32)] + [g.astype(F32) for g in got]
        while len(terms) > 1:
            terms = [sum(terms[k : k + 2]) for k in range(0, len(terms), 2)]
        mine = terms[0]
    other = swap(mine, lambda i: i ^ 1)
    total = call_place(mine, other, float(rows * ways) ** -0.5, bits, filters.shape)
    return gated, grad_projected, total


def solution(mesh):
    placed = (P(("groups", "seq"), None), P(), P(("groups", "seq"), None))
    return jax.shard_map(
        shards,
        mesh=mesh,
        in_specs=placed,
        out_specs=(P(("groups", "seq"), None), P(("groups", "seq"), None), P("groups", None, None)),
        check_vma=False,
    )
```

```python
import functools

import jax
import jax.numpy as jnp
from jax import lax
from jax.experimental import pallas as pl
from jax.experimental.pallas import tpu as pltpu
from jax.sharding import PartitionSpec as P

F32 = jnp.float32
BF = jnp.bfloat16
LANES = 128
SUB = 8
RIM = 8
REACH = 6
VMEM = pl.BlockSpec(memory_space=pltpu.VMEM)
HBM = pl.BlockSpec(memory_space=pltpu.HBM)
UNROLL = 4
RIM_UNROLL = 4


def lanes_at(start):
    return pl.ds(pl.multiple_of(start, LANES), LANES)


def tap_rows(filters, s, n):
    return [
        jnp.broadcast_to(filters[s, j : j + 1, lanes_at(n * LANES)], (SUB, LANES))
        for j in range(filters.shape[1])
    ]


def convolve(tap, slab, s, n, start):
    return sum(tap[j] * slab[s, n, start - j : start - j + SUB, :] for j in range(len(tap)))


def gates(query, key, value, cotangent):
    product = key * value
    scaled = cotangent * query
    grads = (cotangent * product, scaled * value, scaled * key)
    return query * product, [g.astype(BF).astype(F32) for g in grads]


def inner_kernel(p_ref, u_hbm, filters, gated, grads, sums, p_slab, u_ref, u_slab, sem):
    rows, columns = p_ref.shape
    chans = columns // 3
    taps = filters.shape[1]
    fetch = pltpu.make_async_copy(u_hbm, u_ref, sem)
    fetch.start()

    def filter_group(n, carry):
        for s in range(3):
            p_slab[s, n] = p_ref[:, lanes_at(s * chans + n * LANES)].astype(F32)
            tap = tap_rows(filters, s, n)
            for r in range(RIM, rows, SUB):
                grads[s, n, r : r + SUB, :] = convolve(tap, p_slab, s, n, r)
        return carry

    def gate_group(n, carry):
        u_slab[...] = u_ref[:, lanes_at(n * LANES)].astype(F32)
        for r in range(RIM, rows, SUB):
            conv = [grads[s, n, r : r + SUB, :] for s in range(3)]
            product, grad = gates(*conv, u_slab[r : r + SUB, :])
            gated[n, r : r + SUB, :] = product
            for s in range(3):
                grads[s, n, r : r + SUB, :] = grad[s]
        for s in range(3):
            acc = [None] * taps
            for r in range(RIM, rows, SUB):
                grad = grads[s, n, r : r + SUB, :]
                for j in range(taps):
                    term = grad * p_slab[s, n, r - j : r - j + SUB, :]
                    acc[j] = term if r == RIM else acc[j] + term
            for j in range(taps):
                sums[n, s, j] = acc[j]
        return carry

    groups = chans // LANES
    lax.fori_loop(0, groups, filter_group, 0, unroll=UNROLL)
    fetch.wait()
    lax.fori_loop(0, groups, gate_group, 0, unroll=UNROLL)


def fold(arrays):
    sub = lax.broadcasted_iota(jnp.int32, (SUB, LANES), 0)
    arrays = arrays + [jnp.zeros((SUB, LANES), F32)] * (SUB - len(arrays))
    step = 1
    while step < SUB:
        low = (sub & step) == 0
        arrays = [
            jnp.where(low, a, b) + pltpu.roll(jnp.where(low, b, a), SUB - step, 0)
            for a, b in zip(arrays[::2], arrays[1::2])
        ]
        step *= 2
    return arrays[0]


def own_half(bits):
    me = lax.axis_index("seq")
    return lax.rem(sum(lax.rem(me // 2**b, 2) for b in range(bits)), 2)


def rim_kernel(bits, own, p_ref, u_head, filters, before, sums, gated, head, totals, slab):
    _, columns = p_ref.shape
    chans = columns // 3
    taps = filters.shape[1]
    half = chans // 2 // LANES
    first = half * (own_half(bits) if own else 1 - own_half(bits))

    def group(m, carry):
        n = first + m
        for s in range(3):
            c = lanes_at(s * chans + n * LANES)
            slab[s, 0, 0:RIM, :] = pltpu.roll(before[:, c].astype(F32), RIM - REACH, 0)
            slab[s, 0, RIM : RIM + 16, :] = p_ref[0:16, c].astype(F32)
        conv = [convolve(tap_rows(filters, s, n), slab, s, 0, RIM) for s in range(3)]
        product, grad = gates(*conv, u_head[:, lanes_at(n * LANES)].astype(F32)[0:RIM])
        gated[m] = product
        for s in range(3):
            head[s, m] = grad[s]
            acc = [sums[n, s, j] + grad[s] * slab[s, 0, RIM - j : RIM - j + SUB, :] for j in range(taps)]
            totals[pl.ds(s * taps * half + m, taps, stride=half), :] = fold(acc)[:taps]
        return carry

    lax.fori_loop(0, half, group, 0, unroll=RIM_UNROLL)


def next_kernel(p_ref, filters, after, following, slab):
    rows, columns = p_ref.shape
    chans = columns // 3
    sub = lax.broadcasted_iota(jnp.int32, (SUB, LANES), 0)

    def group(n, carry):
        cotangent = jnp.zeros((SUB, LANES), F32)
        for s in range(3):
            c = lanes_at(s * chans + n * LANES)
            tile = after[:, c].astype(F32)
            slab[s, 0, 0:16, :] = p_ref[rows - 16 : rows, c].astype(F32)
            slab[s, 0, 16 : 16 + RIM, :] = tile
            cotangent = jnp.where(sub == s, pltpu.roll(tile, s + 2, 0), cotangent)
            cotangent = jnp.where(sub == s + 3, pltpu.roll(tile, s + 4, 0), cotangent)
        conv = [convolve(tap_rows(filters, s, n), slab, s, 0, 16) for s in range(3)]
        _, grad = gates(*conv, cotangent)
        for s in range(3):
            following[s, n] = grad[s]
        return carry

    lax.fori_loop(0, chans // LANES, group, 0, unroll=UNROLL)


def back_kernel(bits, filters, gated_in, grads, own_gated, own_head, other_gated, other_head, following, gated, out, slab, gated_slab, out_slab, sems):
    rows, columns = out.shape
    chans = columns // 3
    taps = filters.shape[1]
    half = chans // 2 // LANES
    mine = own_half(bits)

    def round_gated(n, carry):
        c = lanes_at(n * LANES)
        gated_slab[0:16, c] = jnp.concatenate([jnp.where(n // half == mine, own_gated[lax.rem(n, half)], other_gated[lax.rem(n, half)]), gated_in[n, RIM:16, :]], 0).astype(BF)
        gated_slab[16:rows, c] = gated_in[n, 16:rows, :].astype(BF)
        return carry

    copies = [pltpu.make_async_copy(gated_slab, gated, sems.at[3])]
    for s in range(3):
        copies.append(pltpu.make_async_copy(out_slab.at[s], out.at[:, s * chans : (s + 1) * chans], sems.at[s]))

    lax.fori_loop(0, chans // LANES, round_gated, 0, unroll=UNROLL)
    copies[0].start()
    for s in range(3):

        def group(n, carry, s=s):
            tap = tap_rows(filters, s, n)
            m = lax.rem(n, half)
            slab[s, 0:RIM, :] = jnp.where(n // half == mine, own_head[s, m], other_head[s, m])
            slab[s, RIM : 2 * RIM, :] = grads[s, n, RIM : 2 * RIM, :]
            slab[s, 2 * RIM : 3 * RIM, :] = grads[s, n, rows - RIM : rows, :]
            slab[s, 3 * RIM : 4 * RIM, :] = following[s, n]
            result = []
            for r in range(0, rows, SUB):
                if r == 0:
                    terms = [tap[j] * slab[s, j : j + SUB, :] for j in range(taps)]
                elif r == rows - SUB:
                    terms = [tap[j] * slab[s, 2 * RIM + j : 2 * RIM + j + SUB, :] for j in range(taps)]
                else:
                    terms = [tap[j] * grads[s, n, r + j : r + j + SUB, :] for j in range(taps)]
                result.append(sum(terms))
                if r % 16 == SUB:
                    out_slab[s, r - SUB : r + SUB, lanes_at(n * LANES)] = jnp.concatenate(result, 0).astype(BF)
                    result = []
            return carry

        lax.fori_loop(0, chans // LANES, group, 0, unroll=UNROLL)
        copies[s + 1].start()
    for copy in copies:
        copy.wait()


def in_hbm(array):
    return pltpu.with_memory_space_constraint(array, pltpu.HBM)


def params(**kw):
    return pltpu.CompilerParams(vmem_limit_bytes=28 * 2**20, **kw)


def call_inner(projected, upstream, filters):
    rows, columns = projected.shape
    chans = columns // 3
    groups = chans // LANES
    taps = filters.shape[1]
    return pl.pallas_call(
        inner_kernel,
        out_shape=(
            jax.ShapeDtypeStruct((groups, rows, LANES), F32),
            jax.ShapeDtypeStruct((3, groups, rows, LANES), F32),
            jax.ShapeDtypeStruct((groups, 3, taps, SUB, LANES), F32),
        ),
        in_specs=[VMEM, HBM, VMEM],
        out_specs=(VMEM,) * 3,
        scratch_shapes=[
            pltpu.VMEM((3, groups, rows, LANES), F32),
            pltpu.VMEM((rows, chans), BF),
            pltpu.VMEM((rows, LANES), F32),
            pltpu.SemaphoreType.DMA,
        ],
        cost_estimate=pl.CostEstimate(flops=4 * taps * rows * columns, bytes_accessed=2 * rows * (columns + chans), transcendentals=0),
        compiler_params=params(),
        name="inner",
    )(projected, in_hbm(upstream), filters)


def call_rim(bits, own, projected, u_head, filters, before, sums):
    half = u_head.shape[1] // 2 // LANES
    taps = filters.shape[1]
    return pl.pallas_call(
        functools.partial(rim_kernel, bits, own),
        out_shape=(
            jax.ShapeDtypeStruct((half, RIM, LANES), F32),
            jax.ShapeDtypeStruct((3, half, RIM, LANES), F32),
            jax.ShapeDtypeStruct((3 * taps * half, LANES), F32),
        ),
        in_specs=[VMEM] * 5,
        out_specs=(VMEM,) * 3,
        scratch_shapes=[pltpu.VMEM((3, 1, RIM + 16, LANES), F32)],
        compiler_params=params(),
        name="rim_own" if own else "rim_other",
    )(projected, u_head, filters, before, sums)


def call_next(projected, filters, after):
    groups = filters.shape[2] // LANES
    return pl.pallas_call(
        next_kernel,
        out_shape=jax.ShapeDtypeStruct((3, groups, RIM, LANES), F32),
        in_specs=[VMEM] * 3,
        out_specs=VMEM,
        scratch_shapes=[pltpu.VMEM((3, 1, 16 + RIM, LANES), F32)],
        compiler_params=params(),
        name="next",
    )(projected, filters, after)


def place_kernel(scale, bits, mine, other, out):
    _, taps, chans = out.shape
    half = chans // 2 // LANES
    odd = own_half(bits)
    for s in range(3):
        for n in range(half):
            place = pl.ds(s * taps * half + n, taps, stride=half)
            out[s, :, lanes_at((odd * half + n) * LANES)] = mine[place, :] * scale
            out[s, :, lanes_at(((1 - odd) * half + n) * LANES)] = other[place, :] * scale


def call_place(mine, other, scale, bits, shape):
    return pl.pallas_call(
        functools.partial(place_kernel, scale, bits),
        out_shape=jax.ShapeDtypeStruct(shape, F32),
        in_specs=[VMEM] * 2,
        out_specs=VMEM,
        compiler_params=params(),
        name="place",
    )(mine, other)


def call_back(bits, filters, gated, grads, *edges):
    taps = filters.shape[1]
    groups, rows, _ = gated.shape
    chans = groups * LANES
    return pl.pallas_call(
        functools.partial(back_kernel, bits),
        out_shape=(jax.ShapeDtypeStruct((rows, chans), BF), jax.ShapeDtypeStruct((rows, 3 * chans), BF)),
        in_specs=[VMEM] * 8,
        out_specs=(HBM,) * 2,
        scratch_shapes=[
            pltpu.VMEM((3, 4 * RIM, LANES), F32),
            pltpu.VMEM((rows, chans), BF),
            pltpu.VMEM((3, rows, chans), BF),
            pltpu.SemaphoreType.DMA((4,)),
        ],
        cost_estimate=pl.CostEstimate(flops=6 * taps * rows * chans, bytes_accessed=8 * rows * chans, transcendentals=0),
        compiler_params=params(),
        name="back",
    )(filters, gated, grads, *edges)

def rounds(bits):
    return [[(1 << b) ^ 1] for b in reversed(range(3, bits))] + [[m for m in (3, 5, 6) if m < 1 << bits]]


def pack_kernel(p_ref, u_ref, u_head, near, far, ends, sems):
    rows, columns = p_ref.shape
    copies = [
        pltpu.make_async_copy(p_ref.at[0:16], ends.at[0:16], sems.at[0]),
        pltpu.make_async_copy(p_ref.at[rows - 16 : rows], ends.at[16:32], sems.at[1]),
        pltpu.make_async_copy(u_ref.at[0:16], u_head, sems.at[2]),
    ]
    for copy in copies:
        copy.start()
    for copy in copies:
        copy.wait()
    forward_near = lax.rem(lax.axis_index("seq"), 2) == 0
    chans = columns // 3
    sub = lax.broadcasted_iota(jnp.int32, (SUB, LANES), 0)

    def group(n, carry):
        cotangent = u_head[:, lanes_at(n * LANES)].astype(F32)[:RIM]
        for s in range(3):
            c = lanes_at(s * chans + n * LANES)
            last = pltpu.roll(ends[16:32, c].astype(F32)[16 - RIM :], REACH, 0)
            first = ends[0:16, c].astype(F32)[:RIM]
            first = jnp.where(sub == 6, pltpu.roll(cotangent, 6 - s, 0), first)
            first = jnp.where(sub == 7, pltpu.roll(cotangent, 4 - s, 0), first)
            near[:, c] = jnp.where(forward_near, last, first).astype(BF)
            far[:, c] = jnp.where(forward_near, first, last).astype(BF)
        return carry

    lax.fori_loop(0, chans // LANES, group, 0, unroll=UNROLL)


def call_pack(projected, upstream):
    columns = projected.shape[1]
    shape = jax.ShapeDtypeStruct((RIM, columns), BF)
    return pl.pallas_call(
        pack_kernel,
        out_shape=(jax.ShapeDtypeStruct((16, upstream.shape[1]), BF), shape, shape),
        in_specs=[HBM] * 2,
        out_specs=(VMEM,) * 3,
        scratch_shapes=[pltpu.VMEM((32, columns), BF), pltpu.SemaphoreType.DMA((3,))],
        compiler_params=params(),
        name="pack",
    )(in_hbm(projected), in_hbm(upstream))


def swap(array, partner):
    ways = lax.axis_size("seq")
    return lax.ppermute(array, "seq", [(i, partner(i)) for i in range(ways)])


def trade_far(array):
    groups, ways = lax.axis_size("groups"), lax.axis_size("seq")

    def partner(g, i):
        if i not in (0, ways - 1):
            return g, ((i + 1) ^ 1) - 1
        return (g ^ 1, i) if groups % 2 == 0 else (g, ways - 1 - i)

    places = [(g, i) for g in range(groups) for i in range(ways)]
    pairs = [(g * ways + i, partner(g, i)[0] * ways + partner(g, i)[1]) for g, i in places]
    return lax.ppermute(array, ("groups", "seq"), pairs)


def rims(projected, upstream):
    ways = lax.axis_size("seq")
    me = lax.axis_index("seq")
    even = me % 2 == 0
    u_head, near, far = call_pack(projected, upstream)
    far = trade_far(far)
    near = swap(near, lambda i: i ^ 1)
    before = jnp.where(even, far, near)
    after = jnp.where(even, near, far)
    before = jnp.where(me == 0, jnp.zeros_like(before), before)
    after = jnp.where(me == ways - 1, jnp.zeros_like(after), after)
    return u_head, before, after


def shards(projected, filters, upstream):
    rows = projected.shape[0]
    ways = lax.axis_size("seq")
    u_head, before, after = rims(projected, upstream)
    gated, grads, sums = call_inner(projected, upstream, filters)
    bits = ways.bit_length() - 1
    *other_edges, sent = call_rim(bits, False, projected, u_head, filters, before, sums)
    sent, before = lax.optimization_barrier((sent, before))
    got = swap(sent, lambda i: i ^ 1)
    *own_edges, mine = call_rim(bits, True, projected, u_head, filters, before, sums)
    got, mine = lax.optimization_barrier((got, mine))
    mine = mine + got
    steps = rounds(bits)
    for step, masks in enumerate(steps):
        sent = mine.astype(BF)
        if step == 0:
            sent, after = lax.optimization_barrier((sent, after))
        if step == len(steps) - 1:
            sent, grads = lax.optimization_barrier((sent, grads))
        got = [swap(sent, lambda i: i ^ m) for m in masks]
        if step == 0:
            following = call_next(projected, filters, after)
            got, following = lax.optimization_barrier((got, following))
        if step == len(steps) - 1:
            gated, grad_projected = call_back(bits, filters, gated, grads, *own_edges, *other_edges, following)
            got, gated, grad_projected = lax.optimization_barrier((got, gated, grad_projected))
        terms = [sent.astype(F32)] + [g.astype(F32) for g in got]
        while len(terms) > 1:
            terms = [sum(terms[k : k + 2]) for k in range(0, len(terms), 2)]
        mine = terms[0]
    other = swap(mine, lambda i: i ^ 1)
    total = call_place(mine, other, float(rows * ways) ** -0.5, bits, filters.shape)
    return gated, grad_projected, total


def solution(mesh):
    placed = (P(("groups", "seq"), None), P(), P(("groups", "seq"), None))
    return jax.shard_map(
        shards,
        mesh=mesh,
        in_specs=placed,
        out_specs=(P(("groups", "seq"), None), P(("groups", "seq"), None), P("groups", None, None)),
        check_vma=False,
    )
```

```python
import functools

import jax
import jax.numpy as jnp
from jax import lax
from jax.experimental import pallas as pl
from jax.experimental.pallas import tpu as pltpu
from jax.sharding import PartitionSpec as P

F32 = jnp.float32
BF = jnp.bfloat16
LANES = 128
SUB = 8
RIM = 8
REACH = 6
VMEM = pl.BlockSpec(memory_space=pltpu.VMEM)
HBM = pl.BlockSpec(memory_space=pltpu.HBM)
UNROLL = 4
RIM_UNROLL = 4


def lanes_at(start):
    return pl.ds(pl.multiple_of(start, LANES), LANES)


def tap_rows(filters, s, n):
    return [
        jnp.broadcast_to(filters[s, j : j + 1, lanes_at(n * LANES)], (SUB, LANES))
        for j in range(filters.shape[1])
    ]


def convolve(tap, slab, s, n, start):
    return sum(tap[j] * slab[s, n, start - j : start - j + SUB, :] for j in range(len(tap)))


def gates(query, key, value, cotangent):
    product = key * value
    scaled = cotangent * query
    grads = (cotangent * product, scaled * value, scaled * key)
    return query * product, [g.astype(BF).astype(F32) for g in grads]


def inner_kernel(p_ref, u_hbm, filters, gated, grads, sums, p_slab, u_ref, u_slab, sem):
    rows, columns = p_ref.shape
    chans = columns // 3
    taps = filters.shape[1]
    fetch = pltpu.make_async_copy(u_hbm, u_ref, sem)
    fetch.start()

    def filter_group(n, carry):
        for s in range(3):
            p_slab[s, n] = p_ref[:, lanes_at(s * chans + n * LANES)].astype(F32)
            tap = tap_rows(filters, s, n)
            for r in range(RIM, rows, SUB):
                grads[s, n, r : r + SUB, :] = convolve(tap, p_slab, s, n, r)
        return carry

    def gate_group(n, carry):
        u_slab[...] = u_ref[:, lanes_at(n * LANES)].astype(F32)
        for r in range(RIM, rows, SUB):
            conv = [grads[s, n, r : r + SUB, :] for s in range(3)]
            product, grad = gates(*conv, u_slab[r : r + SUB, :])
            gated[n, r : r + SUB, :] = product
            for s in range(3):
                grads[s, n, r : r + SUB, :] = grad[s]
        for s in range(3):
            acc = [None] * taps
            for r in range(RIM, rows, SUB):
                grad = grads[s, n, r : r + SUB, :]
                for j in range(taps):
                    term = grad * p_slab[s, n, r - j : r - j + SUB, :]
                    acc[j] = term if r == RIM else acc[j] + term
            for j in range(taps):
                sums[n, s, j] = acc[j]
        return carry

    groups = chans // LANES
    lax.fori_loop(0, groups, filter_group, 0, unroll=UNROLL)
    fetch.wait()
    lax.fori_loop(0, groups, gate_group, 0, unroll=UNROLL)


def fold(arrays):
    sub = lax.broadcasted_iota(jnp.int32, (SUB, LANES), 0)
    arrays = arrays + [jnp.zeros((SUB, LANES), F32)] * (SUB - len(arrays))
    step = 1
    while step < SUB:
        low = (sub & step) == 0
        arrays = [
            jnp.where(low, a, b) + pltpu.roll(jnp.where(low, b, a), SUB - step, 0)
            for a, b in zip(arrays[::2], arrays[1::2])
        ]
        step *= 2
    return arrays[0]


def own_half(bits):
    me = lax.axis_index("seq")
    return lax.rem(sum(lax.rem(me // 2**b, 2) for b in range(bits)), 2)


def rim_kernel(bits, own, p_ref, u_head, filters, before, sums, gated, head, totals, slab, wide):
    _, columns = p_ref.shape
    chans = columns // 3
    taps = filters.shape[1]
    half = chans // 2 // LANES
    first = half * (own_half(bits) if own else 1 - own_half(bits))

    def group(m, carry):
        n = first + m
        for s in range(3):
            c = lanes_at(s * chans + n * LANES)
            slab[s, 0, 0:RIM, :] = pltpu.roll(before[:, c].astype(F32), RIM - REACH, 0)
            slab[s, 0, RIM : RIM + 16, :] = p_ref[0:16, c].astype(F32)
        conv = [convolve(tap_rows(filters, s, n), slab, s, 0, RIM) for s in range(3)]
        product, grad = gates(*conv, u_head[:, lanes_at(n * LANES)].astype(F32)[0:RIM])
        gated[m] = product
        for s in range(3):
            head[s, m] = grad[s]
            acc = [sums[n, s, j] + grad[s] * slab[s, 0, RIM - j : RIM - j + SUB, :] for j in range(taps)]
            wide[pl.ds(s * SUB * half + m, SUB, stride=half), :] = fold(acc)
        return carry

    lax.fori_loop(0, half, group, 0, unroll=RIM_UNROLL)
    for s in range(3):
        totals[s * taps * half : (s + 1) * taps * half, :] = wide[s * SUB * half : (s * SUB + taps) * half, :]


def next_kernel(p_ref, filters, after, following, slab):
    rows, columns = p_ref.shape
    chans = columns // 3
    sub = lax.broadcasted_iota(jnp.int32, (SUB, LANES), 0)

    def group(n, carry):
        cotangent = jnp.zeros((SUB, LANES), F32)
        for s in range(3):
            c = lanes_at(s * chans + n * LANES)
            tile = after[:, c].astype(F32)
            slab[s, 0, 0:16, :] = p_ref[rows - 16 : rows, c].astype(F32)
            slab[s, 0, 16 : 16 + RIM, :] = tile
            cotangent = jnp.where(sub == s, pltpu.roll(tile, s + 2, 0), cotangent)
            cotangent = jnp.where(sub == s + 3, pltpu.roll(tile, s + 4, 0), cotangent)
        conv = [convolve(tap_rows(filters, s, n), slab, s, 0, 16) for s in range(3)]
        _, grad = gates(*conv, cotangent)
        for s in range(3):
            following[s, n] = grad[s]
        return carry

    lax.fori_loop(0, chans // LANES, group, 0, unroll=UNROLL)


def back_kernel(bits, filters, gated_in, grads, own_gated, own_head, other_gated, other_head, following, gated, out, slab, gated_slab, out_slab, sems):
    rows, columns = out.shape
    chans = columns // 3
    taps = filters.shape[1]
    half = chans // 2 // LANES
    mine = own_half(bits)

    def round_gated(n, carry):
        c = lanes_at(n * LANES)
        gated_slab[0:16, c] = jnp.concatenate([jnp.where(n // half == mine, own_gated[lax.rem(n, half)], other_gated[lax.rem(n, half)]), gated_in[n, RIM:16, :]], 0).astype(BF)
        gated_slab[16:rows, c] = gated_in[n, 16:rows, :].astype(BF)
        return carry

    copies = [pltpu.make_async_copy(gated_slab, gated, sems.at[3])]
    for s in range(3):
        copies.append(pltpu.make_async_copy(out_slab.at[s], out.at[:, s * chans : (s + 1) * chans], sems.at[s]))

    lax.fori_loop(0, chans // LANES, round_gated, 0, unroll=UNROLL)
    copies[0].start()
    for s in range(3):

        def group(n, carry, s=s):
            tap = tap_rows(filters, s, n)
            m = lax.rem(n, half)
            slab[s, 0:RIM, :] = jnp.where(n // half == mine, own_head[s, m], other_head[s, m])
            slab[s, RIM : 2 * RIM, :] = grads[s, n, RIM : 2 * RIM, :]
            slab[s, 2 * RIM : 3 * RIM, :] = grads[s, n, rows - RIM : rows, :]
            slab[s, 3 * RIM : 4 * RIM, :] = following[s, n]
            result = []
            for r in range(0, rows, SUB):
                if r == 0:
                    terms = [tap[j] * slab[s, j : j + SUB, :] for j in range(taps)]
                elif r == rows - SUB:
                    terms = [tap[j] * slab[s, 2 * RIM + j : 2 * RIM + j + SUB, :] for j in range(taps)]
                else:
                    terms = [tap[j] * grads[s, n, r + j : r + j + SUB, :] for j in range(taps)]
                result.append(sum(terms))
                if r % 16 == SUB:
                    out_slab[s, r - SUB : r + SUB, lanes_at(n * LANES)] = jnp.concatenate(result, 0).astype(BF)
                    result = []
            return carry

        lax.fori_loop(0, chans // LANES, group, 0, unroll=UNROLL)
        copies[s + 1].start()
    for copy in copies:
        copy.wait()


def in_hbm(array):
    return pltpu.with_memory_space_constraint(array, pltpu.HBM)


def params(**kw):
    return pltpu.CompilerParams(vmem_limit_bytes=28 * 2**20, **kw)


def call_inner(projected, upstream, filters):
    rows, columns = projected.shape
    chans = columns // 3
    groups = chans // LANES
    taps = filters.shape[1]
    return pl.pallas_call(
        inner_kernel,
        out_shape=(
            jax.ShapeDtypeStruct((groups, rows, LANES), F32),
            jax.ShapeDtypeStruct((3, groups, rows, LANES), F32),
            jax.ShapeDtypeStruct((groups, 3, taps, SUB, LANES), F32),
        ),
        in_specs=[VMEM, HBM, VMEM],
        out_specs=(VMEM,) * 3,
        scratch_shapes=[
            pltpu.VMEM((3, groups, rows, LANES), F32),
            pltpu.VMEM((rows, chans), BF),
            pltpu.VMEM((rows, LANES), F32),
            pltpu.SemaphoreType.DMA,
        ],
        cost_estimate=pl.CostEstimate(flops=4 * taps * rows * columns, bytes_accessed=2 * rows * (columns + chans), transcendentals=0),
        compiler_params=params(),
        name="inner",
    )(projected, in_hbm(upstream), filters)


def call_rim(bits, own, projected, u_head, filters, before, sums):
    half = u_head.shape[1] // 2 // LANES
    taps = filters.shape[1]
    return pl.pallas_call(
        functools.partial(rim_kernel, bits, own),
        out_shape=(
            jax.ShapeDtypeStruct((half, RIM, LANES), F32),
            jax.ShapeDtypeStruct((3, half, RIM, LANES), F32),
            jax.ShapeDtypeStruct((3 * taps * half, LANES), F32),
        ),
        in_specs=[VMEM] * 5,
        out_specs=(VMEM,) * 3,
        scratch_shapes=[
            pltpu.VMEM((3, 1, RIM + 16, LANES), F32),
            pltpu.VMEM((3 * SUB * half, LANES), F32),
        ],
        compiler_params=params(),
        name="rim_own" if own else "rim_other",
    )(projected, u_head, filters, before, sums)


def call_next(projected, filters, after):
    groups = filters.shape[2] // LANES
    return pl.pallas_call(
        next_kernel,
        out_shape=jax.ShapeDtypeStruct((3, groups, RIM, LANES), F32),
        in_specs=[VMEM] * 3,
        out_specs=VMEM,
        scratch_shapes=[pltpu.VMEM((3, 1, 16 + RIM, LANES), F32)],
        compiler_params=params(),
        name="next",
    )(projected, filters, after)


def place_kernel(scale, bits, mine, other, out, wide):
    _, taps, chans = out.shape
    half = chans // 2 // LANES
    odd = own_half(bits)
    for k, (array, side) in enumerate(((mine, odd), (other, 1 - odd))):
        for s in range(3):
            wide[k, s * SUB * half : (s * SUB + taps) * half, :] = array[s * taps * half : (s + 1) * taps * half, :]
            for n in range(half):
                tile = wide[k, pl.ds(s * SUB * half + n, SUB, stride=half), :]
                out[s, :, lanes_at((side * half + n) * LANES)] = tile[:taps] * scale


def call_place(mine, other, scale, bits, shape):
    return pl.pallas_call(
        functools.partial(place_kernel, scale, bits),
        out_shape=jax.ShapeDtypeStruct(shape, F32),
        in_specs=[VMEM] * 2,
        out_specs=VMEM,
        scratch_shapes=[pltpu.VMEM((2, 3 * SUB * (shape[2] // 2 // LANES), LANES), F32)],
        compiler_params=params(),
        name="place",
    )(mine, other)


def call_back(bits, filters, gated, grads, *edges):
    taps = filters.shape[1]
    groups, rows, _ = gated.shape
    chans = groups * LANES
    return pl.pallas_call(
        functools.partial(back_kernel, bits),
        out_shape=(jax.ShapeDtypeStruct((rows, chans), BF), jax.ShapeDtypeStruct((rows, 3 * chans), BF)),
        in_specs=[VMEM] * 8,
        out_specs=(HBM,) * 2,
        scratch_shapes=[
            pltpu.VMEM((3, 4 * RIM, LANES), F32),
            pltpu.VMEM((rows, chans), BF),
            pltpu.VMEM((3, rows, chans), BF),
            pltpu.SemaphoreType.DMA((4,)),
        ],
        cost_estimate=pl.CostEstimate(flops=6 * taps * rows * chans, bytes_accessed=8 * rows * chans, transcendentals=0),
        compiler_params=params(),
        name="back",
    )(filters, gated, grads, *edges)

def rounds(bits):
    return [[(1 << b) ^ 1] for b in reversed(range(3, bits))] + [[m for m in (3, 5, 6) if m < 1 << bits]]


def pack_kernel(p_ref, u_ref, u_head, near, far, ends, sems):
    rows, columns = p_ref.shape
    copies = [
        pltpu.make_async_copy(p_ref.at[0:16], ends.at[0:16], sems.at[0]),
        pltpu.make_async_copy(p_ref.at[rows - 16 : rows], ends.at[16:32], sems.at[1]),
        pltpu.make_async_copy(u_ref.at[0:16], u_head, sems.at[2]),
    ]
    for copy in copies:
        copy.start()
    for copy in copies:
        copy.wait()
    forward_near = lax.rem(lax.axis_index("seq"), 2) == 0
    chans = columns // 3
    sub = lax.broadcasted_iota(jnp.int32, (SUB, LANES), 0)

    def group(n, carry):
        cotangent = u_head[:, lanes_at(n * LANES)].astype(F32)[:RIM]
        for s in range(3):
            c = lanes_at(s * chans + n * LANES)
            last = pltpu.roll(ends[16:32, c].astype(F32)[16 - RIM :], REACH, 0)
            first = ends[0:16, c].astype(F32)[:RIM]
            first = jnp.where(sub == 6, pltpu.roll(cotangent, 6 - s, 0), first)
            first = jnp.where(sub == 7, pltpu.roll(cotangent, 4 - s, 0), first)
            near[:, c] = jnp.where(forward_near, last, first).astype(BF)
            far[:, c] = jnp.where(forward_near, first, last).astype(BF)
        return carry

    lax.fori_loop(0, chans // LANES, group, 0, unroll=UNROLL)


def call_pack(projected, upstream):
    columns = projected.shape[1]
    shape = jax.ShapeDtypeStruct((RIM, columns), BF)
    return pl.pallas_call(
        pack_kernel,
        out_shape=(jax.ShapeDtypeStruct((16, upstream.shape[1]), BF), shape, shape),
        in_specs=[HBM] * 2,
        out_specs=(VMEM,) * 3,
        scratch_shapes=[pltpu.VMEM((32, columns), BF), pltpu.SemaphoreType.DMA((3,))],
        compiler_params=params(),
        name="pack",
    )(in_hbm(projected), in_hbm(upstream))


def swap(array, partner):
    ways = lax.axis_size("seq")
    return lax.ppermute(array, "seq", [(i, partner(i)) for i in range(ways)])


def trade_far(array):
    groups, ways = lax.axis_size("groups"), lax.axis_size("seq")

    def partner(g, i):
        if i not in (0, ways - 1):
            return g, ((i + 1) ^ 1) - 1
        return (g ^ 1, i) if groups % 2 == 0 else (g, ways - 1 - i)

    places = [(g, i) for g in range(groups) for i in range(ways)]
    pairs = [(g * ways + i, partner(g, i)[0] * ways + partner(g, i)[1]) for g, i in places]
    return lax.ppermute(array, ("groups", "seq"), pairs)


def rims(projected, upstream):
    ways = lax.axis_size("seq")
    me = lax.axis_index("seq")
    even = me % 2 == 0
    u_head, near, far = call_pack(projected, upstream)
    far = trade_far(far)
    near = swap(near, lambda i: i ^ 1)
    before = jnp.where(even, far, near)
    after = jnp.where(even, near, far)
    before = jnp.where(me == 0, jnp.zeros_like(before), before)
    after = jnp.where(me == ways - 1, jnp.zeros_like(after), after)
    return u_head, before, after


def shards(projected, filters, upstream):
    rows = projected.shape[0]
    ways = lax.axis_size("seq")
    u_head, before, after = rims(projected, upstream)
    gated, grads, sums = call_inner(projected, upstream, filters)
    bits = ways.bit_length() - 1
    *other_edges, sent = call_rim(bits, False, projected, u_head, filters, before, sums)
    sent, before = lax.optimization_barrier((sent, before))
    got = swap(sent, lambda i: i ^ 1)
    *own_edges, mine = call_rim(bits, True, projected, u_head, filters, before, sums)
    got, mine = lax.optimization_barrier((got, mine))
    mine = mine + got
    steps = rounds(bits)
    for step, masks in enumerate(steps):
        sent = mine.astype(BF)
        if step == 0:
            sent, after = lax.optimization_barrier((sent, after))
        if step == len(steps) - 1:
            sent, grads = lax.optimization_barrier((sent, grads))
        got = [swap(sent, lambda i: i ^ m) for m in masks]
        if step == 0:
            following = call_next(projected, filters, after)
            got, following = lax.optimization_barrier((got, following))
        if step == len(steps) - 1:
            gated, grad_projected = call_back(bits, filters, gated, grads, *own_edges, *other_edges, following)
            got, gated, grad_projected = lax.optimization_barrier((got, gated, grad_projected))
        terms = [sent.astype(F32)] + [g.astype(F32) for g in got]
        while len(terms) > 1:
            terms = [sum(terms[k : k + 2]) for k in range(0, len(terms), 2)]
        mine = terms[0]
    other = swap(mine, lambda i: i ^ 1)
    total = call_place(mine, other, float(rows * ways) ** -0.5, bits, filters.shape)
    return gated, grad_projected, total


def solution(mesh):
    placed = (P(("groups", "seq"), None), P(), P(("groups", "seq"), None))
    return jax.shard_map(
        shards,
        mesh=mesh,
        in_specs=placed,
        out_specs=(P(("groups", "seq"), None), P(("groups", "seq"), None), P("groups", None, None)),
        check_vma=False,
    )
```

```python
import functools

import jax
import jax.numpy as jnp
from jax import lax
from jax.experimental import pallas as pl
from jax.experimental.pallas import tpu as pltpu
from jax.sharding import PartitionSpec as P

F32 = jnp.float32
BF = jnp.bfloat16
LANES = 128
SUB = 8
RIM = 8
REACH = 6
VMEM = pl.BlockSpec(memory_space=pltpu.VMEM)
HBM = pl.BlockSpec(memory_space=pltpu.HBM)
UNROLL = 8
RIM_UNROLL = 8


def lanes_at(start):
    return pl.ds(pl.multiple_of(start, LANES), LANES)


def tap_rows(filters, s, n):
    return [
        jnp.broadcast_to(filters[s, j : j + 1, lanes_at(n * LANES)], (SUB, LANES))
        for j in range(filters.shape[1])
    ]


def convolve(tap, slab, s, n, start):
    return sum(tap[j] * slab[s, n, start - j : start - j + SUB, :] for j in range(len(tap)))


def gates(query, key, value, cotangent):
    product = key * value
    scaled = cotangent * query
    grads = (cotangent * product, scaled * value, scaled * key)
    return query * product, [g.astype(BF).astype(F32) for g in grads]


def inner_kernel(p_ref, u_hbm, filters, gated, grads, sums, p_slab, u_ref, u_slab, sem):
    rows, columns = p_ref.shape
    chans = columns // 3
    taps = filters.shape[1]
    fetch = pltpu.make_async_copy(u_hbm, u_ref, sem)
    fetch.start()

    def filter_group(n, carry):
        for s in range(3):
            p_slab[s, n] = p_ref[:, lanes_at(s * chans + n * LANES)].astype(F32)
            tap = tap_rows(filters, s, n)
            for r in range(RIM, rows, SUB):
                grads[s, n, r : r + SUB, :] = convolve(tap, p_slab, s, n, r)
        return carry

    def gate_group(n, carry):
        u_slab[...] = u_ref[:, lanes_at(n * LANES)].astype(F32)
        for r in range(RIM, rows, SUB):
            conv = [grads[s, n, r : r + SUB, :] for s in range(3)]
            product, grad = gates(*conv, u_slab[r : r + SUB, :])
            gated[n, r : r + SUB, :] = product
            for s in range(3):
                grads[s, n, r : r + SUB, :] = grad[s]
        for s in range(3):
            acc = [None] * taps
            for r in range(RIM, rows, SUB):
                grad = grads[s, n, r : r + SUB, :]
                for j in range(taps):
                    term = grad * p_slab[s, n, r - j : r - j + SUB, :]
                    acc[j] = term if r == RIM else acc[j] + term
            for j in range(taps):
                sums[n, s, j] = acc[j]
        return carry

    groups = chans // LANES
    lax.fori_loop(0, groups, filter_group, 0, unroll=UNROLL)
    fetch.wait()
    lax.fori_loop(0, groups, gate_group, 0, unroll=UNROLL)


def fold(arrays):
    sub = lax.broadcasted_iota(jnp.int32, (SUB, LANES), 0)
    arrays = arrays + [jnp.zeros((SUB, LANES), F32)] * (SUB - len(arrays))
    step = 1
    while step < SUB:
        low = (sub & step) == 0
        arrays = [
            jnp.where(low, a, b) + pltpu.roll(jnp.where(low, b, a), SUB - step, 0)
            for a, b in zip(arrays[::2], arrays[1::2])
        ]
        step *= 2
    return arrays[0]


def own_half(bits):
    me = lax.axis_index("seq")
    return lax.rem(sum(lax.rem(me // 2**b, 2) for b in range(bits)), 2)


def rim_kernel(bits, own, p_ref, u_head, filters, before, sums, gated, head, totals, slab, wide):
    _, columns = p_ref.shape
    chans = columns // 3
    taps = filters.shape[1]
    half = chans // 2 // LANES
    first = half * (own_half(bits) if own else 1 - own_half(bits))

    def group(m, carry):
        n = first + m
        for s in range(3):
            c = lanes_at(s * chans + n * LANES)
            slab[s, 0, 0:RIM, :] = pltpu.roll(before[:, c].astype(F32), RIM - REACH, 0)
            slab[s, 0, RIM : RIM + 16, :] = p_ref[0:16, c].astype(F32)
        conv = [convolve(tap_rows(filters, s, n), slab, s, 0, RIM) for s in range(3)]
        product, grad = gates(*conv, u_head[:, lanes_at(n * LANES)].astype(F32)[0:RIM])
        gated[m] = product
        for s in range(3):
            head[s, m] = grad[s]
            acc = [sums[n, s, j] + grad[s] * slab[s, 0, RIM - j : RIM - j + SUB, :] for j in range(taps)]
            wide[pl.ds(s * SUB * half + m, SUB, stride=half), :] = fold(acc)
        return carry

    lax.fori_loop(0, half, group, 0, unroll=RIM_UNROLL)
    for s in range(3):
        totals[s * taps * half : (s + 1) * taps * half, :] = wide[s * SUB * half : (s * SUB + taps) * half, :]


def next_kernel(p_ref, filters, after, following, slab):
    rows, columns = p_ref.shape
    chans = columns // 3
    sub = lax.broadcasted_iota(jnp.int32, (SUB, LANES), 0)

    def group(n, carry):
        cotangent = jnp.zeros((SUB, LANES), F32)
        for s in range(3):
            c = lanes_at(s * chans + n * LANES)
            tile = after[:, c].astype(F32)
            slab[s, 0, 0:16, :] = p_ref[rows - 16 : rows, c].astype(F32)
            slab[s, 0, 16 : 16 + RIM, :] = tile
            cotangent = jnp.where(sub == s, pltpu.roll(tile, s + 2, 0), cotangent)
            cotangent = jnp.where(sub == s + 3, pltpu.roll(tile, s + 4, 0), cotangent)
        conv = [convolve(tap_rows(filters, s, n), slab, s, 0, 16) for s in range(3)]
        _, grad = gates(*conv, cotangent)
        for s in range(3):
            following[s, n] = grad[s]
        return carry

    lax.fori_loop(0, chans // LANES, group, 0, unroll=UNROLL)


def back_kernel(bits, filters, gated_in, grads, own_gated, own_head, other_gated, other_head, following, gated, out, slab, gated_slab, out_slab, sems):
    rows, columns = out.shape
    chans = columns // 3
    taps = filters.shape[1]
    half = chans // 2 // LANES
    mine = own_half(bits)

    def round_gated(n, carry):
        c = lanes_at(n * LANES)
        gated_slab[0:16, c] = jnp.concatenate([jnp.where(n // half == mine, own_gated[lax.rem(n, half)], other_gated[lax.rem(n, half)]), gated_in[n, RIM:16, :]], 0).astype(BF)
        gated_slab[16:rows, c] = gated_in[n, 16:rows, :].astype(BF)
        return carry

    copies = [pltpu.make_async_copy(gated_slab, gated, sems.at[3])]
    for s in range(3):
        copies.append(pltpu.make_async_copy(out_slab.at[s], out.at[:, s * chans : (s + 1) * chans], sems.at[s]))

    lax.fori_loop(0, chans // LANES, round_gated, 0, unroll=UNROLL)
    copies[0].start()
    for s in range(3):

        def group(n, carry, s=s):
            tap = tap_rows(filters, s, n)
            m = lax.rem(n, half)
            slab[s, 0:RIM, :] = jnp.where(n // half == mine, own_head[s, m], other_head[s, m])
            slab[s, RIM : 2 * RIM, :] = grads[s, n, RIM : 2 * RIM, :]
            slab[s, 2 * RIM : 3 * RIM, :] = grads[s, n, rows - RIM : rows, :]
            slab[s, 3 * RIM : 4 * RIM, :] = following[s, n]
            result = []
            for r in range(0, rows, SUB):
                if r == 0:
                    terms = [tap[j] * slab[s, j : j + SUB, :] for j in range(taps)]
                elif r == rows - SUB:
                    terms = [tap[j] * slab[s, 2 * RIM + j : 2 * RIM + j + SUB, :] for j in range(taps)]
                else:
                    terms = [tap[j] * grads[s, n, r + j : r + j + SUB, :] for j in range(taps)]
                result.append(sum(terms))
                if r % 16 == SUB:
                    out_slab[s, r - SUB : r + SUB, lanes_at(n * LANES)] = jnp.concatenate(result, 0).astype(BF)
                    result = []
            return carry

        lax.fori_loop(0, chans // LANES, group, 0, unroll=UNROLL)
        copies[s + 1].start()
    for copy in copies:
        copy.wait()


def in_hbm(array):
    return pltpu.with_memory_space_constraint(array, pltpu.HBM)


def params(**kw):
    return pltpu.CompilerParams(vmem_limit_bytes=28 * 2**20, **kw)


def call_inner(projected, upstream, filters):
    rows, columns = projected.shape
    chans = columns // 3
    groups = chans // LANES
    taps = filters.shape[1]
    return pl.pallas_call(
        inner_kernel,
        out_shape=(
            jax.ShapeDtypeStruct((groups, rows, LANES), F32),
            jax.ShapeDtypeStruct((3, groups, rows, LANES), F32),
            jax.ShapeDtypeStruct((groups, 3, taps, SUB, LANES), F32),
        ),
        in_specs=[VMEM, HBM, VMEM],
        out_specs=(VMEM,) * 3,
        scratch_shapes=[
            pltpu.VMEM((3, groups, rows, LANES), F32),
            pltpu.VMEM((rows, chans), BF),
            pltpu.VMEM((rows, LANES), F32),
            pltpu.SemaphoreType.DMA,
        ],
        cost_estimate=pl.CostEstimate(flops=4 * taps * rows * columns, bytes_accessed=2 * rows * (columns + chans), transcendentals=0),
        compiler_params=params(),
        name="inner",
    )(projected, in_hbm(upstream), filters)


def call_rim(bits, own, projected, u_head, filters, before, sums):
    half = u_head.shape[1] // 2 // LANES
    taps = filters.shape[1]
    return pl.pallas_call(
        functools.partial(rim_kernel, bits, own),
        out_shape=(
            jax.ShapeDtypeStruct((half, RIM, LANES), F32),
            jax.ShapeDtypeStruct((3, half, RIM, LANES), F32),
            jax.ShapeDtypeStruct((3 * taps * half, LANES), F32),
        ),
        in_specs=[VMEM] * 5,
        out_specs=(VMEM,) * 3,
        scratch_shapes=[
            pltpu.VMEM((3, 1, RIM + 16, LANES), F32),
            pltpu.VMEM((3 * SUB * half, LANES), F32),
        ],
        compiler_params=params(),
        name="rim_own" if own else "rim_other",
    )(projected, u_head, filters, before, sums)


def call_next(projected, filters, after):
    groups = filters.shape[2] // LANES
    return pl.pallas_call(
        next_kernel,
        out_shape=jax.ShapeDtypeStruct((3, groups, RIM, LANES), F32),
        in_specs=[VMEM] * 3,
        out_specs=VMEM,
        scratch_shapes=[pltpu.VMEM((3, 1, 16 + RIM, LANES), F32)],
        compiler_params=params(),
        name="next",
    )(projected, filters, after)


def place_kernel(scale, bits, own, array, *refs):
    out, wide, stage, sem = refs[-4:]
    _, taps, lanes = stage.shape
    half = lanes // LANES
    side = own_half(bits) if own else 1 - own_half(bits)
    for s in range(3):
        wide[s * SUB * half : (s * SUB + taps) * half, :] = array[s * taps * half : (s + 1) * taps * half, :]
        for n in range(half):
            tile = wide[pl.ds(s * SUB * half + n, SUB, stride=half), :]
            stage[s, :, n * LANES : (n + 1) * LANES] = tile[:taps] * scale
    copy = pltpu.make_async_copy(stage, out.at[:, :, pl.ds(pl.multiple_of(side * lanes, LANES), lanes)], sem)
    copy.start()
    copy.wait()


def call_place(own, scale, bits, shape, array, *placed):
    _, taps, chans = shape
    return pl.pallas_call(
        functools.partial(place_kernel, scale, bits, own),
        out_shape=jax.ShapeDtypeStruct(shape, F32),
        in_specs=[VMEM] + [HBM] * len(placed),
        out_specs=HBM,
        input_output_aliases={1: 0} if placed else {},
        scratch_shapes=[
            pltpu.VMEM((3 * SUB * (chans // 2 // LANES), LANES), F32),
            pltpu.VMEM((3, taps, chans // 2), F32),
            pltpu.SemaphoreType.DMA,
        ],
        compiler_params=params(),
        name="place_own" if own else "place_other",
    )(array, *placed)


def call_back(bits, filters, gated, grads, *edges):
    taps = filters.shape[1]
    groups, rows, _ = gated.shape
    chans = groups * LANES
    return pl.pallas_call(
        functools.partial(back_kernel, bits),
        out_shape=(jax.ShapeDtypeStruct((rows, chans), BF), jax.ShapeDtypeStruct((rows, 3 * chans), BF)),
        in_specs=[VMEM] * 8,
        out_specs=(HBM,) * 2,
        scratch_shapes=[
            pltpu.VMEM((3, 4 * RIM, LANES), F32),
            pltpu.VMEM((rows, chans), BF),
            pltpu.VMEM((3, rows, chans), BF),
            pltpu.SemaphoreType.DMA((4,)),
        ],
        cost_estimate=pl.CostEstimate(flops=6 * taps * rows * chans, bytes_accessed=8 * rows * chans, transcendentals=0),
        compiler_params=params(),
        name="back",
    )(filters, gated, grads, *edges)

def rounds(bits):
    return [[(1 << b) ^ 1] for b in reversed(range(3, bits))] + [[m for m in (3, 5, 6) if m < 1 << bits]]


def pack_kernel(p_ref, u_ref, u_head, near, far, ends, sems):
    rows, columns = p_ref.shape
    copies = [
        pltpu.make_async_copy(p_ref.at[0:16], ends.at[0:16], sems.at[0]),
        pltpu.make_async_copy(p_ref.at[rows - 16 : rows], ends.at[16:32], sems.at[1]),
        pltpu.make_async_copy(u_ref.at[0:16], u_head, sems.at[2]),
    ]
    for copy in copies:
        copy.start()
    for copy in copies:
        copy.wait()
    forward_near = lax.rem(lax.axis_index("seq"), 2) == 0
    chans = columns // 3
    sub = lax.broadcasted_iota(jnp.int32, (SUB, LANES), 0)

    def group(n, carry):
        cotangent = u_head[:, lanes_at(n * LANES)].astype(F32)[:RIM]
        for s in range(3):
            c = lanes_at(s * chans + n * LANES)
            last = pltpu.roll(ends[16:32, c].astype(F32)[16 - RIM :], REACH, 0)
            first = ends[0:16, c].astype(F32)[:RIM]
            first = jnp.where(sub == 6, pltpu.roll(cotangent, 6 - s, 0), first)
            first = jnp.where(sub == 7, pltpu.roll(cotangent, 4 - s, 0), first)
            near[:, c] = jnp.where(forward_near, last, first).astype(BF)
            far[:, c] = jnp.where(forward_near, first, last).astype(BF)
        return carry

    lax.fori_loop(0, chans // LANES, group, 0, unroll=UNROLL)


def call_pack(projected, upstream):
    columns = projected.shape[1]
    shape = jax.ShapeDtypeStruct((RIM, columns), BF)
    return pl.pallas_call(
        pack_kernel,
        out_shape=(jax.ShapeDtypeStruct((16, upstream.shape[1]), BF), shape, shape),
        in_specs=[HBM] * 2,
        out_specs=(VMEM,) * 3,
        scratch_shapes=[pltpu.VMEM((32, columns), BF), pltpu.SemaphoreType.DMA((3,))],
        compiler_params=params(),
        name="pack",
    )(in_hbm(projected), in_hbm(upstream))


def swap(array, partner):
    ways = lax.axis_size("seq")
    return lax.ppermute(array, "seq", [(i, partner(i)) for i in range(ways)])


def trade_far(array):
    groups, ways = lax.axis_size("groups"), lax.axis_size("seq")

    def partner(g, i):
        if i not in (0, ways - 1):
            return g, ((i + 1) ^ 1) - 1
        return (g ^ 1, i) if groups % 2 == 0 else (g, ways - 1 - i)

    places = [(g, i) for g in range(groups) for i in range(ways)]
    pairs = [(g * ways + i, partner(g, i)[0] * ways + partner(g, i)[1]) for g, i in places]
    return lax.ppermute(array, ("groups", "seq"), pairs)


def rims(projected, upstream):
    ways = lax.axis_size("seq")
    me = lax.axis_index("seq")
    even = me % 2 == 0
    u_head, near, far = call_pack(projected, upstream)
    far = trade_far(far)
    near = swap(near, lambda i: i ^ 1)
    before = jnp.where(even, far, near)
    after = jnp.where(even, near, far)
    before = jnp.where(me == 0, jnp.zeros_like(before), before)
    after = jnp.where(me == ways - 1, jnp.zeros_like(after), after)
    return u_head, before, after


def shards(projected, filters, upstream):
    rows = projected.shape[0]
    ways = lax.axis_size("seq")
    u_head, before, after = rims(projected, upstream)
    gated, grads, sums = call_inner(projected, upstream, filters)
    bits = ways.bit_length() - 1
    *other_edges, sent = call_rim(bits, False, projected, u_head, filters, before, sums)
    sent, before = lax.optimization_barrier((sent, before))
    got = swap(sent, lambda i: i ^ 1)
    *own_edges, mine = call_rim(bits, True, projected, u_head, filters, before, sums)
    got, mine = lax.optimization_barrier((got, mine))
    mine = mine + got
    steps = rounds(bits)
    for step, masks in enumerate(steps):
        sent = mine.astype(BF)
        if step == 0:
            sent, after = lax.optimization_barrier((sent, after))
        if step == len(steps) - 1:
            sent, grads = lax.optimization_barrier((sent, grads))
        got = [swap(sent, lambda i: i ^ m) for m in masks]
        if step == 0:
            following = call_next(projected, filters, after)
            got, following = lax.optimization_barrier((got, following))
        if step == len(steps) - 1:
            gated, grad_projected = call_back(bits, filters, gated, grads, *own_edges, *other_edges, following)
            got, gated, grad_projected = lax.optimization_barrier((got, gated, grad_projected))
        terms = [sent.astype(F32)] + [g.astype(F32) for g in got]
        while len(terms) > 1:
            terms = [sum(terms[k : k + 2]) for k in range(0, len(terms), 2)]
        mine = terms[0]
    scale = float(rows * ways) ** -0.5
    other = swap(mine, lambda i: i ^ 1)
    total = call_place(True, scale, bits, filters.shape, mine)
    other, total = lax.optimization_barrier((other, total))
    total = call_place(False, scale, bits, filters.shape, other, total)
    return gated, grad_projected, total


def solution(mesh):
    placed = (P(("groups", "seq"), None), P(), P(("groups", "seq"), None))
    return jax.shard_map(
        shards,
        mesh=mesh,
        in_specs=placed,
        out_specs=(P(("groups", "seq"), None), P(("groups", "seq"), None), P("groups", None, None)),
        check_vma=False,
    )
```
